256 devices in a mesh: seq: 32 (over y, x, core), head: 4 (over z_lo), grp: 2 (over z_hi).
Axes of the slice: x: 4, y: 4, z: 8 (z_hi: 2, z_lo: 4; z = z_hi * 4 + z_lo), core: 2. Of those that a mesh axis runs over, the one named last changes fastest.
Arguments:
- queries: bfloat16 [32768, 8192], P(('seq', 'grp'), 'head'), may hold values from -6 to 6
- keys: bfloat16 [32768, 1024], P(('seq', 'grp'), 'head'), may hold values from -6 to 6
- values: bfloat16 [32768, 1024], P(('seq', 'grp'), 'head'), may hold values from -10 to 10
- memory_init: float32 [8, 128, 128], P('head'), may hold values from -256 to 256
- norm_init: float32 [8, 128], P('head'), may hold values from 16 to 64
- gate_logits: float32 [64], replicated, may hold values from -2.5 to 2.5
- dec_queries: bfloat16 [512, 3, 8192], P(('seq', 'head', 'grp')), may hold values from -6 to 6
- cache_keys: bfloat16 [512, 512, 1024], P(('seq', 'head', 'grp')), may hold values from -6 to 6
- cache_values: bfloat16 [512, 512, 1024], P(('seq', 'head', 'grp')), may hold values from -6 to 6
- new_keys: bfloat16 [512, 3, 1024], P(('seq', 'head', 'grp')), may hold values from -6 to 6
- new_values: bfloat16 [512, 3, 1024], P(('seq', 'head', 'grp')), may hold values from -6 to 6
- cache_lengths: int32 [512], P(('seq', 'head', 'grp')), may hold values from 2 to 512, as said below
Outputs:
- prefill_out: bfloat16 [32768, 8192], P(('seq', 'grp'), 'head')
- decode_out: bfloat16 [512, 3, 8192], P(('seq', 'head', 'grp'))
The draws below stay inside these ranges and needn't reach their ends.
Inputs may be any that keep to these rules, and one draw needn't show every extreme that they name: `cache_lengths`: at least one request has exactly 512 live slots.
All inputs are finite; a program needn't handle non-finite values.
Results may differ from the reference program's by a relative error of at most 0.0045.
Values may be sent and summed in bfloat16 or wider, within the bound.
A program may use at most 128 MiB of HBM per device.

```python
import math
import jax
import jax.numpy as jnp
from jax import lax

QH = 64
KVH = 8
HD = 128
SEG = 1024
STEPS = 3
CACHE = 512
TOKENS = 32768
REQ = 512


query_lift = 4.0


topic_weight = 1.5


def shuffle_dims(sub_key):
    return jax.random.permutation(sub_key, HD)


def topic_plan(key):
    key = jax.random.fold_in(key, 404)
    first, second, third = jax.random.split(key, 3)
    dim_topic = jax.vmap(shuffle_dims)(jax.random.split(first, KVH))
    token_topic = jax.random.randint(second, (TOKENS, KVH), 0, HD)
    table = jnp.clip(jax.random.normal(third, (HD, KVH, HD), jnp.float32), -2.0, 2.0)
    return (dim_topic, token_topic, table)


def memory_norms(key):
    key = jax.random.fold_in(key, 303)
    return SEG * jnp.exp(jax.random.uniform(key, (KVH, HD), jnp.float32, math.log(1.0 / 64.0), math.log(1.0 / 16.0)))


def draw_queries(key, part):
    anchor = key
    dim_topic, token_topic, table = topic_plan(anchor)
    key = jax.random.fold_in(key, 1)
    first, second = jax.random.split(key)
    owner = jnp.arange(QH) // (QH // KVH)
    query_topic = jax.random.randint(second, (TOKENS, QH), 0, HD)
    lifted = (dim_topic[owner][None, :, :] == query_topic[:, :, None]).astype(jnp.float32)
    drawn = jnp.clip(jax.random.normal(first, (TOKENS, QH, HD), jnp.float32) + query_lift * lifted, -6.0, 6.0)
    return drawn.reshape(TOKENS, QH * HD).astype(jnp.bfloat16)


def draw_keys(key, part):
    anchor = key
    dim_topic, token_topic, table = topic_plan(anchor)
    key = jax.random.fold_in(key, 2)
    first, second = jax.random.split(key)
    segments = TOKENS // SEG
    ramp = jnp.arange(segments).astype(jnp.float32) / max(segments - 1, 1)
    places = jnp.arange(TOKENS)
    segment = places // SEG
    floor_level = -5.0 + ramp
    spike_level = 1.0 + 4.5 * ramp
    shifts = jax.random.uniform(second, (segments, KVH, HD), jnp.float32, -0.5, 0.5)
    lifted = dim_topic[None, :, :] == token_topic[:, :, None]
    center = jnp.where(lifted, spike_level[segment][:, None, None], floor_level[segment][:, None, None] + shifts[segment])
    drawn = jnp.clip(jax.random.normal(first, (TOKENS, KVH, HD), jnp.float32) + center, -6.0, 6.0)
    return drawn.reshape(TOKENS, KVH * HD).astype(jnp.bfloat16)


def draw_values(key, part):
    anchor = key
    dim_topic, token_topic, table = topic_plan(anchor)
    key = jax.random.fold_in(key, 3)
    first, second = jax.random.split(key)
    segments = TOKENS // SEG
    noise = jnp.clip(jax.random.normal(first, (TOKENS, KVH * HD), jnp.float32), -4.0, 4.0)
    offset = jnp.clip(jax.random.normal(second, (segments, KVH * HD), jnp.float32), -2.0, 2.0)
    ramp = jnp.arange(segments).astype(jnp.float32) / max(segments - 1, 1)
    later = jnp.arange(TOKENS) % SEG >= SEG // 2
    growth = 0.5 + 1.5 * ramp
    halves = jnp.where(later, 1.5, 0.5)
    carried = table[token_topic, jnp.arange(KVH)[None, :]].reshape(TOKENS, KVH * HD)
    drawn = noise + jnp.repeat(offset * growth[:, None], SEG, axis=0) + topic_weight * carried
    drawn = drawn * halves[:, None]
    return jnp.clip(drawn, -10.0, 10.0).astype(jnp.bfloat16)


def draw_memory_init(key, part):
    norms = memory_norms(key)
    key = jax.random.fold_in(key, 4)
    first, second = jax.random.split(key)
    center = jnp.clip(jax.random.normal(first, (KVH, 1, HD), jnp.float32), -2.0, 2.0)
    noise = 0.5 * jnp.clip(jax.random.normal(second, (KVH, HD, HD), jnp.float32), -4.0, 4.0)
    return (norms[:, :, None] * (center + noise)).astype(jnp.float32)


def draw_norm_init(key, part):
    norms = memory_norms(key)
    return norms.astype(jnp.float32)


def draw_dec_queries(key, part):
    anchor = key
    dim_topic, token_topic, table = topic_plan(anchor)
    key = jax.random.fold_in(key, 6)
    first, second = jax.random.split(key)
    owner = jnp.arange(QH) // (QH // KVH)
    query_topic = jax.random.randint(second, (REQ, STEPS, QH), 0, HD)
    lifted = (dim_topic[owner][None, None, :, :] == query_topic[:, :, :, None]).astype(jnp.float32)
    drawn = jnp.clip(jax.random.normal(first, (REQ, STEPS, QH, HD), jnp.float32) + query_lift * lifted, -6.0, 6.0)
    return drawn.reshape(REQ, STEPS, QH * HD).astype(jnp.bfloat16)


def draw_cache_keys(key, part):
    key = jax.random.fold_in(key, 7)
    drawn = jnp.clip(jax.random.normal(key, (REQ, CACHE, KVH, HD), jnp.float32), -6.0, 6.0)
    return drawn.reshape(REQ, CACHE, KVH * HD).astype(jnp.bfloat16)


def draw_cache_lengths(key, part):
    key = jax.random.fold_in(key, 8)
    first, second = jax.random.split(key)
    lengths = jax.random.randint(first, (REQ,), 2, CACHE + 1)
    fullest = jax.random.randint(second, (), 0, REQ)
    return jnp.where(jnp.arange(REQ) == fullest, CACHE, lengths).astype(jnp.int32)


def steps_of(key, extent, pieces, least, top_value):
    gain, own = 1.0, jax.random.fold_in(key, 6)
    for position, blocks in pieces:
        draws = jnp.exp(jax.random.uniform(jax.random.fold_in(own, position), (blocks,), jnp.float32, least / len(pieces), top_value / len(pieces)))
        gain = gain * jnp.repeat(draws, extent[position] // blocks).reshape([-1 if axis == position else 1 for axis in range(len(extent))])
    return gain


def normal_values(own_key, extent, width, most, shards=(), held_as=jnp.bfloat16):
    entries = width * jax.random.normal(own_key, extent, jnp.float32)
    if shards:
        entries = entries * steps_of(own_key, extent, shards, -0.22, 0.18)
    return jnp.clip(entries, -most, most).astype(held_as)


def setup_inputs(seed: int = 0) -> dict:
    key_of = jax.random.split(jax.random.key(seed), 13)
    queries = draw_queries(jax.random.fold_in(key_of[12], 71), 0)
    keys = draw_keys(jax.random.fold_in(key_of[12], 71), 0)
    values = draw_values(jax.random.fold_in(key_of[12], 71), 0)
    memory_init = draw_memory_init(jax.random.fold_in(key_of[12], 71), 0)
    norm_init = draw_norm_init(jax.random.fold_in(key_of[12], 71), 0)
    gate_logits = jnp.clip(jax.random.uniform(key_of[5], (QH,), jnp.float32, -2.5, 2.5), -2.5, 2.5)
    dec_queries = draw_dec_queries(jax.random.fold_in(key_of[12], 71), 0)
    cache_keys = draw_cache_keys(jax.random.fold_in(key_of[12], 71), 0)
    cache_values = normal_values(key_of[8], (REQ, CACHE, KVH * HD), 1.0, 6.0, ((0, 256),))
    new_keys = normal_values(key_of[9], (REQ, STEPS, KVH * HD), 1.0, 6.0, ((0, 256),))
    new_values = normal_values(key_of[10], (REQ, STEPS, KVH * HD), 1.0, 6.0, ((0, 256),))
    cache_lengths = draw_cache_lengths(jax.random.fold_in(key_of[12], 71), 0)
    return dict(queries=queries, keys=keys, values=values, memory_init=memory_init, norm_init=norm_init, gate_logits=gate_logits, dec_queries=dec_queries, cache_keys=cache_keys, cache_values=cache_values, new_keys=new_keys, new_values=new_values, cache_lengths=cache_lengths)


def feature_map(values_in):
    widened = values_in.astype(jnp.float32)
    return jnp.where(widened > 0, widened + 1.0, jnp.exp(jnp.minimum(widened, 0.0)))

def rounded(weights):
    return lax.optimization_barrier(weights.astype(jnp.bfloat16)).astype(jnp.float32)

def retrieve(lifted, memory, norm_vec):
    numer = jnp.einsum('...kgd,kde->...kge', lifted, memory, precision=lax.Precision.HIGHEST)
    denom = jnp.einsum('...kgd,kd->...kg', lifted, norm_vec, precision=lax.Precision.HIGHEST)
    return numer / denom[..., None]

def reference(queries, keys, values, memory_init, norm_init, gate_logits, dec_queries, cache_keys, cache_values, new_keys, new_values, cache_lengths):
    segments = TOKENS // SEG
    group = QH // KVH
    scale = 1.0 / math.sqrt(HD)
    gates = jax.nn.sigmoid(gate_logits).reshape(KVH, group)[:, :, None]
    key_split = keys.reshape(segments, SEG, KVH, HD)
    value_split = values.reshape(segments, SEG, KVH, HD)
    lifted_keys = rounded(feature_map(key_split))
    parts = jnp.einsum('nskd,nske->nkde', lifted_keys, value_split.astype(jnp.float32))
    sums = lax.optimization_barrier(jnp.sum(lifted_keys, axis=1))
    prior_memory = memory_init[None] + jnp.concatenate([jnp.zeros((1, KVH, HD, HD), jnp.float32), jnp.cumsum(parts, axis=0)[:-1]], axis=0)
    prior_norm = norm_init[None] + jnp.concatenate([jnp.zeros((1, KVH, HD), jnp.float32), jnp.cumsum(sums, axis=0)[:-1]], axis=0)
    query_split = queries.reshape(segments, SEG, KVH, group, HD)
    places = jnp.arange(SEG)
    causal = places[:, None] >= places[None, :]

    def one_segment(items):
        query_one, key_one, value_one, memory, norm_vec = items
        scores = jnp.einsum('qkgd,skd->kgqs', query_one.astype(jnp.float32), key_one.astype(jnp.float32)) * scale
        scores = jnp.where(causal, scores, -1e+30)
        highest = lax.optimization_barrier(jnp.max(scores, axis=-1, keepdims=True))
        weights = jnp.exp(scores - highest)
        total = lax.optimization_barrier(jnp.sum(weights, axis=-1))
        local = jnp.einsum('kgqs,skd->qkgd', rounded(weights), value_one.astype(jnp.float32))
        local = local / jnp.transpose(total, (2, 0, 1))[..., None]
        memory_part = retrieve(feature_map(query_one), memory, norm_vec)
        mixed = gates * memory_part + (1.0 - gates) * local
        return mixed.reshape(SEG, QH * HD).astype(jnp.bfloat16)
    prefill_out = lax.map(one_segment, (query_split, key_split, value_split, prior_memory, prior_norm)).reshape(TOKENS, QH * HD)
    total_memory = memory_init + lax.optimization_barrier(jnp.sum(parts, axis=0))
    total_norm = norm_init + lax.optimization_barrier(jnp.sum(sums, axis=0))
    step_mask = jnp.arange(STEPS)[:, None] >= jnp.arange(STEPS)[None, :]
    slots = jnp.arange(CACHE).astype(jnp.int32)

    def one_request(items):
        query_one, cached_key, cached_value, fresh_key, fresh_value, length = items
        query_wide = query_one.astype(jnp.float32).reshape(STEPS, KVH, group, HD)
        cached_key = cached_key.astype(jnp.float32).reshape(CACHE, KVH, HD)
        cached_value = cached_value.astype(jnp.float32).reshape(CACHE, KVH, HD)
        fresh_key = fresh_key.astype(jnp.float32).reshape(STEPS, KVH, HD)
        fresh_value = fresh_value.astype(jnp.float32).reshape(STEPS, KVH, HD)
        cache_scores = jnp.einsum('tkgd,skd->kgts', query_wide, cached_key) * scale
        cache_scores = jnp.where((slots < length)[None, None, None, :], cache_scores, -1e+30)
        fresh_scores = jnp.einsum('tkgd,ukd->kgtu', query_wide, fresh_key) * scale
        fresh_scores = jnp.where(step_mask, fresh_scores, -1e+30)
        highest = jnp.maximum(lax.optimization_barrier(jnp.max(cache_scores, axis=-1)), lax.optimization_barrier(jnp.max(fresh_scores, axis=-1)))[..., None]
        cache_weights = jnp.exp(cache_scores - highest)
        fresh_weights = jnp.exp(fresh_scores - highest)
        total = lax.optimization_barrier(jnp.sum(cache_weights, axis=-1)) + lax.optimization_barrier(jnp.sum(fresh_weights, axis=-1))
        local = jnp.einsum('kgts,skd->tkgd', rounded(cache_weights), cached_value) + jnp.einsum('kgtu,ukd->tkgd', rounded(fresh_weights), fresh_value)
        local = local / jnp.transpose(total, (2, 0, 1))[..., None]
        memory_part = retrieve(feature_map(query_one).reshape(STEPS, KVH, group, HD), total_memory, total_norm)
        mixed = gates * memory_part + (1.0 - gates) * local
        return mixed.reshape(STEPS, QH * HD).astype(jnp.bfloat16)
    decode_out = lax.map(one_request, (dec_queries, cache_keys, cache_values, new_keys, new_values, cache_lengths))
    return (prefill_out, decode_out)
```

```python
import functools
import math

import jax
import jax.numpy as jnp
from jax import lax
from jax.experimental import pallas as pl
from jax.experimental.pallas import tpu as pltpu
from jax.sharding import PartitionSpec as P

MESH = pl.DeviceIdType.MESH
BF = jnp.bfloat16
F32 = jnp.float32

D = 128
ROWS = 512
G = 8
KH = 2
NK = 8
STEPS = 3
CACHE = 512
OWN = 8
YS = 4
HEADS = 4
SL = D // OWN
B1 = KH * SL + 16
B2 = KH * SL + 8
B4 = KH * D + 16
LOG2E = 1.4426950408889634
C = LOG2E / math.sqrt(D)
NEG = -1e30


def dot(a, b):
    return lax.dot_general(a, b, (((1,), (0,)), ((), ())), preferred_element_type=F32)


def dot_nt(a, b):
    return lax.dot_general(a, b, (((1,), (1,)), ((), ())), preferred_element_type=F32)


def dot_tn(a, b):
    return lax.dot_general(a, b, (((0,), (0,)), ((), ())), preferred_element_type=F32)


def lift(x):
    return jnp.where(x > 0, x + 1.0, jnp.exp(jnp.minimum(x, 0.0)))


def split(x):
    hi = x.astype(BF)
    return hi, (x - hi.astype(F32)).astype(BF)


def inverse(x):
    r = pl.reciprocal(x, approx=True)
    r = r * (2.0 - x * r)
    return r * (2.0 - x * r)


def lanes(s):
    return [s[:, i * D : (i + 1) * D] for i in range(s.shape[1] // D)]


def row_max(tiles):
    top = functools.reduce(jnp.maximum, tiles)
    return jnp.broadcast_to(jnp.max(top, axis=1, keepdims=True), top.shape)


def weights_of(tiles, top):
    shift = top * C
    return jnp.concatenate([jnp.exp2(t * C - shift).astype(BF) for t in tiles], axis=1)


def kernel(
    q_hbm, k_hbm, v_hbm, mem_init, norm_init, gates, dq, ck_hbm, cv_hbm, nk, nv, lengths,
    out_hbm, dec_out,
    q, k, vx, ke, vxe, ck, cv, out,
    acc, den, top, ret,
    gm, gd, qd, nf, fk, fv, dloc,
    snd1, r1, snd2, r2, snd3, r3, snd4, r4, prior, pnorm,
    lsem, osem, kvs, kvr, s1, rs1, s2, rs2, s3, rs3, s4, rs4,
):
    seq = lax.axis_index("seq")
    head = lax.axis_index("head")
    grp = lax.axis_index("grp")
    y = seq // OWN
    o = seq % OWN
    me = grp * OWN + o

    loads = []
    for j in range(KH):
        cols = pl.ds(j * D, D)
        loads.append(pltpu.make_async_copy(k_hbm.at[:, cols], k.at[j], lsem.at[j]))
        loads.append(pltpu.make_async_copy(v_hbm.at[:, cols], vx.at[j, :, 0:D], lsem.at[KH + j]))
    load_q = pltpu.make_async_copy(q_hbm, q, lsem.at[4])
    load_ck = pltpu.make_async_copy(ck_hbm, ck, lsem.at[5])
    load_cv = pltpu.make_async_copy(cv_hbm, cv, lsem.at[6])
    for copy in loads:
        copy.start()
    load_q.start()
    load_ck.start()
    load_cv.start()

    def ring_peer(n):
        t = (me + n) % (2 * OWN)
        return {"seq": y * OWN + t % OWN, "grp": t // OWN}

    def y_peer(n):
        return {"seq": ((y + n) % YS) * OWN + o}

    def head_peer(n):
        return {"head": (head + n) % HEADS}

    barrier = pltpu.get_barrier_semaphore()
    for n in range(1, 2 * OWN):
        pl.semaphore_signal(barrier, inc=1, device_id=ring_peer(n), device_id_type=MESH)
    for n in range(1, YS):
        pl.semaphore_signal(barrier, inc=1, device_id=y_peer(n), device_id_type=MESH)
    for n in range(1, HEADS):
        pl.semaphore_signal(barrier, inc=1, device_id=head_peer(n), device_id_type=MESH)

    for j in range(KH):
        vx[j, :, D:] = jnp.ones((ROWS, D), BF)
        vxe[j, :, D:] = jnp.ones((ROWS, D), BF)
    for copy in loads:
        copy.wait()

    row16 = lax.broadcasted_iota(jnp.int32, (16, D), 0)
    norm_rows = jnp.zeros((16, D), F32)
    for j in range(KH):
        lifted = lift(k[j].astype(F32)).astype(BF)
        part = dot_tn(lifted, vx[j, :, 0:D]).astype(BF)
        for t in range(OWN):
            snd1[t, j * SL : (j + 1) * SL, :] = part[t * SL : (t + 1) * SL]
        norm_rows = norm_rows + jnp.where(
            row16 == j, dot(jnp.ones((16, ROWS), BF), lifted), 0.0
        )
    for t in range(OWN):
        snd1[t, KH * SL :, :] = norm_rows.astype(BF)
    r1[me] = snd1[o]

    pl.semaphore_wait(barrier, 2 * OWN - 1 + YS - 1 + HEADS - 1)

    def send1(n):
        t = (me + n) % (2 * OWN)
        return pltpu.make_async_remote_copy(
            snd1.at[t % OWN], r1.at[me], s1.at[n], rs1.at[n], device_id=ring_peer(n), device_id_type=MESH
        )

    def recv1(n):
        f = (me + 2 * OWN - n) % (2 * OWN)
        return pltpu.make_async_remote_copy(
            snd1.at[o], r1.at[f], s1.at[n], rs1.at[n], device_id=ring_peer(n), device_id_type=MESH
        )

    for n in range(1, 2 * OWN):
        send1(n).start()

    def kv_copy(j, what):
        src, dst = (k.at[j], ke.at[j]) if what == 0 else (vx.at[j, :, 0:D], vxe.at[j, :, 0:D])
        return pltpu.make_async_remote_copy(
            src, dst, kvs.at[2 * j + what], kvr.at[2 * j + what],
            device_id={"grp": 1 - grp}, device_id_type=MESH,
        )

    @pl.when(grp == 0)
    def _():
        for j in range(KH):
            kv_copy(j, 0).start()
            kv_copy(j, 1).start()

    logits = gates[...]
    sig = 1.0 / (1.0 + jnp.exp(-logits))
    at = lax.broadcasted_iota(jnp.int32, (NK * G, NK * G), 0)
    col = lax.broadcasted_iota(jnp.int32, (NK * G, NK * G), 1)
    gm[...] = jnp.broadcast_to(
        jnp.sum(jnp.where(at == col, sig, 0.0), axis=1, keepdims=True), (NK * G, D)
    )
    at = lax.broadcasted_iota(jnp.int32, (NK * G * 4, NK * G), 0)
    col = lax.broadcasted_iota(jnp.int32, (NK * G * 4, NK * G), 1)
    own_row = (at >= col * 4) & (at < col * 4 + 4)
    gd[...] = jnp.broadcast_to(
        jnp.sum(jnp.where(own_row, sig, 0.0), axis=1, keepdims=True), (NK * G * 4, D)
    )

    load_q.wait()

    half = ROWS // 2
    r_at = lax.broadcasted_iota(jnp.int32, (half, D), 0)
    c_at = lax.broadcasted_iota(jnp.int32, (half, D), 1)

    def own_rows(j):
        def one(gi, _):
            h = j * G + gi
            lane = pl.ds(pl.multiple_of(h * D, D), D)
            for b in range(2):
                rows = pl.ds(b * half, half)
                q_one = q[rows, lane]
                tiles = lanes(dot_nt(q_one, k[j, 0 : (b + 1) * half, :]))
                n = len(tiles)
                for i in range(2):
                    keep = c_at + i * D <= r_at
                    tiles[n - 2 + i] = jnp.where(keep, tiles[n - 2 + i], NEG)
                m = row_max(tiles)
                w = weights_of(tiles, m)
                res = dot(w, vx[j, 0 : (b + 1) * half, :])
                acc[h, rows, :] = res[:, :D]
                den[h, rows, :] = res[:, D:]
                top[h, rows, :] = m
            return 0

        lax.fori_loop(0, G, one, 0)

    own_rows(0)

    for n in range(1, 2 * OWN):
        recv1(n).wait_recv()
    run = jnp.zeros((B2, D), F32)
    for t in range(OWN):
        snd3[t, 0:B2, :] = run
        run = run + (r1[t].astype(F32) + r1[OWN + t].astype(F32))[:B2]
    snd2[...] = run
    r2[y] = run

    def send2(n):
        return pltpu.make_async_remote_copy(
            snd2, r2.at[y], s2.at[n], rs2.at[n], device_id=y_peer(n), device_id_type=MESH
        )

    def recv2(n):
        return pltpu.make_async_remote_copy(
            snd2, r2.at[(y + YS - n) % YS], s2.at[n], rs2.at[n], device_id=y_peer(n), device_id_type=MESH
        )

    for n in range(1, YS):
        send2(n).start()

    own_rows(1)

    for n in range(1, YS):
        recv2(n).wait_recv()
    base = jnp.zeros((B2, D), F32)
    total = jnp.zeros((B2, D), F32)
    for t in range(YS):
        base = base + jnp.where(t < y, r2[t], 0.0)
        total = total + r2[t]
    for t in range(OWN):
        snd3[t, 0:B2, :] = snd3[t, 0:B2, :] + base
        snd3[t, B2 : 2 * B2, :] = total
    r3[o] = snd3[o]

    def row_peer(n):
        return {"seq": y * OWN + (o + n) % OWN}

    def send3(n):
        return pltpu.make_async_remote_copy(
            snd3.at[(o + n) % OWN], r3.at[o], s3.at[n], rs3.at[n], device_id=row_peer(n), device_id_type=MESH
        )

    def recv3(n):
        return pltpu.make_async_remote_copy(
            snd3.at[o], r3.at[(o + OWN - n) % OWN], s3.at[n], rs3.at[n],
            device_id=row_peer(n), device_id_type=MESH,
        )

    for n in range(1, OWN):
        send3(n).start()

    qd[...] = jnp.zeros_like(qd)
    fk[...] = jnp.zeros_like(fk)
    fv[...] = jnp.zeros_like(fv)
    nf[...] = jnp.zeros_like(nf)
    for r in range(2):
        for j in range(NK):
            for gi in range(G):
                at_h = (j * G + gi) * D
                qd[r, j, gi * 4 : gi * 4 + STEPS, :] = dq[r, :, at_h : at_h + D].astype(F32)
        nf[0:STEPS, :] = nk[r].astype(F32)
        fk[r, 0:16, :] = nf[...].astype(BF)
        nf[0:STEPS, :] = nv[r].astype(F32)
        fv[r, 0:16, :] = nf[...].astype(BF)
    load_ck.wait()
    load_cv.wait()

    c64 = lax.broadcasted_iota(jnp.int32, (64, D), 1)
    t64 = lax.broadcasted_iota(jnp.int32, (64, D), 0) % 4
    fresh_ok = (c64 <= t64) & (c64 < STEPS)

    def decode(r):
        length = lengths[r]

        def one(p, _):
            lane = pl.ds(pl.multiple_of(p * 2 * D, 2 * D), 2 * D)
            none = jnp.zeros((32, D), BF)
            q0 = qd[r, 2 * p].astype(BF)
            q1 = qd[r, 2 * p + 1].astype(BF)
            both = jnp.concatenate(
                [jnp.concatenate([q0, none], axis=1), jnp.concatenate([none, q1], axis=1)], axis=0
            )
            tiles = lanes(dot_nt(both, ck[r, :, lane]))
            tiles = [jnp.where(c64 + i * D < length, s, NEG) for i, s in enumerate(tiles)]
            tiles.append(jnp.where(fresh_ok, dot_nt(both, fk[r, :, lane]), NEG))
            shift = row_max(tiles) * C
            ws = [jnp.exp2(s * C - shift) for s in tiles]
            tot = jnp.sum(functools.reduce(jnp.add, ws), axis=1, keepdims=True)
            ws = [w.astype(BF) for w in ws]
            res = dot(jnp.concatenate(ws[:-1], axis=1), cv[r, :, lane]) + dot(ws[-1], fv[r, :, lane])
            res = res / tot
            dloc[r, 2 * p] = res[0:32, 0:D]
            dloc[r, 2 * p + 1] = res[32:64, D:]
            return 0

        lax.fori_loop(0, NK // 2, one, 0)

    decode(0)

    for n in range(1, OWN):
        recv3(n).wait_recv()
    for j in range(KH):
        for t in range(OWN):
            at_d = pl.ds(t * SL, SL)
            init = mem_init[j, at_d, :]
            prior[j, at_d, :] = r3[t, j * SL : (j + 1) * SL, :] + init
            snd4[j * D + t * SL : j * D + (t + 1) * SL, :] = (
                r3[t, B2 + j * SL : B2 + (j + 1) * SL, :] + init
            ).astype(BF)
    norms = r3[0, KH * SL : B2, :]
    norms_all = r3[0, B2 + KH * SL : 2 * B2, :]
    row8 = lax.broadcasted_iota(jnp.int32, (8, D), 0)
    init8 = jnp.zeros((8, D), F32)
    for j in range(KH):
        init8 = init8 + jnp.where(row8 == j, norm_init[j : j + 1, :], 0.0)
    pnorm[...] = norms + init8
    snd4[KH * D :, :] = jnp.concatenate([norms_all + init8, jnp.zeros((8, D), F32)], axis=0).astype(BF)
    r4[head] = snd4[...]

    def send4(n):
        return pltpu.make_async_remote_copy(
            snd4, r4.at[head], s4.at[n], rs4.at[n], device_id=head_peer(n), device_id_type=MESH
        )

    def recv4(n):
        return pltpu.make_async_remote_copy(
            snd4, r4.at[(head + HEADS - n) % HEADS], s4.at[n], rs4.at[n],
            device_id=head_peer(n), device_id_type=MESH,
        )

    for n in range(1, HEADS):
        send4(n).start()

    decode(1)

    for j in range(KH):
        m_hi, m_lo = split(prior[j])
        wide = jnp.concatenate([m_hi, m_lo], axis=1)
        numer_w = jnp.concatenate([wide, wide], axis=0)
        n_hi, n_lo = split(jnp.broadcast_to(pnorm[j : j + 1, :], (D, D)))
        tall = jnp.concatenate([n_hi, n_lo], axis=0)
        denom_w = jnp.concatenate([tall, tall], axis=1)

        def one(gi, _, j=j, numer_w=numer_w, denom_w=denom_w):
            h = j * G + gi
            lane = pl.ds(pl.multiple_of(h * D, D), D)
            gate = gm[pl.ds(head * KH * G + h, 1), :]
            for b in range(2):
                rows = pl.ds(b * half, half)
                hi, lo = split(lift(q[rows, lane].astype(F32)))
                pair = jnp.concatenate([hi, lo], axis=1)
                numer = dot(pair, numer_w)
                denom = dot_nt(pair, denom_w)
                ret[h, rows, :] = (
                    (numer[:, :D] + numer[:, D:]) * inverse(denom[:, :D] + denom[:, D:]) * gate
                )
            return 0

        lax.fori_loop(0, G, one, 0)

    for n in range(1, HEADS):
        recv4(n).wait_recv()
    for j in range(NK):
        m_one = r4[j // KH, (j % KH) * D : (j % KH + 1) * D, :]
        numer_w = jnp.concatenate([m_one, m_one], axis=0)
        n_rows = r4[j // KH, KH * D :, :].astype(F32)
        n_one = jnp.broadcast_to(n_rows[j % KH : j % KH + 1, :], (D, D)).astype(BF)
        denom_w = jnp.concatenate([n_one, n_one], axis=1)
        x = jnp.concatenate([qd[0, j], qd[1, j]], axis=0)
        hi, lo = split(lift(x))
        pair = jnp.concatenate([hi, lo], axis=1)
        got = dot(pair, numer_w) * inverse(dot_nt(pair, denom_w))
        gate = gd[j * G * 4 : (j + 1) * G * 4, :]
        for r in range(2):
            mixed = gate * got[r * 32 : (r + 1) * 32] + (1.0 - gate) * dloc[r, j]
            for gi in range(G):
                at_h = (j * G + gi) * D
                dec_out[r, :, at_h : at_h + D] = mixed[gi * 4 : gi * 4 + STEPS].astype(BF)

    def out_copy(j):
        cols = pl.ds(j * G * D, G * D)
        return pltpu.make_async_copy(out.at[:, cols], out_hbm.at[:, cols], osem.at[j])

    def finish(j, later):
        def one(gi, _):
            h = j * G + gi
            lane = pl.ds(pl.multiple_of(h * D, D), D)
            gate = gm[pl.ds(head * KH * G + h, 1), :]
            for b in range(2):
                rows = pl.ds(b * half, half)
                if later:
                    tiles = lanes(dot_nt(q[rows, lane], ke[j]))
                    m_own = top[h, rows, :]
                    m = jnp.maximum(row_max(tiles), m_own)
                    res = dot(weights_of(tiles, m), vxe[j])
                    fade = jnp.exp2((m_own - m) * C)
                    numer = acc[h, rows, :] * fade + res[:, :D]
                    denom = den[h, rows, :] * fade + res[:, D:]
                else:
                    numer = acc[h, rows, :]
                    denom = den[h, rows, :]
                out[rows, lane] = (
                    ret[h, rows, :] + (1.0 - gate) * numer * inverse(denom)
                ).astype(BF)
            return 0

        lax.fori_loop(0, G, one, 0)

    @pl.when(grp == 1)
    def _():
        for j in range(KH):
            kv_copy(j, 0).wait_recv()
            kv_copy(j, 1).wait_recv()
            finish(j, True)
            out_copy(j).start()

    @pl.when(grp == 0)
    def _():
        for j in range(KH):
            finish(j, False)
            out_copy(j).start()
        for j in range(KH):
            kv_copy(j, 0).wait_send()
            kv_copy(j, 1).wait_send()

    for n in range(1, 2 * OWN):
        send1(n).wait_send()
    for n in range(1, YS):
        send2(n).wait_send()
    for n in range(1, OWN):
        send3(n).wait_send()
    for n in range(1, HEADS):
        send4(n).wait_send()
    for j in range(KH):
        out_copy(j).wait()


def on_device(
    queries, keys, values, memory_init, norm_init, gate_logits,
    dec_queries, cache_keys, cache_values, new_keys, new_values, cache_lengths,
):
    hbm = pl.BlockSpec(memory_space=pl.ANY)
    vmem = pl.BlockSpec(memory_space=pltpu.VMEM)
    smem = pl.BlockSpec(memory_space=pltpu.SMEM)
    V = pltpu.VMEM
    DMA = pltpu.SemaphoreType.DMA
    return pl.pallas_call(
        kernel,
        out_shape=(
            jax.ShapeDtypeStruct((ROWS, KH * G * D), BF),
            jax.ShapeDtypeStruct((2, STEPS, NK * G * D), BF),
        ),
        in_specs=[hbm, hbm, hbm, vmem, vmem, vmem, vmem, hbm, hbm, vmem, vmem, smem],
        out_specs=(hbm, vmem),
        scratch_shapes=[
            V((ROWS, KH * G * D), BF),
            V((KH, ROWS, D), BF),
            V((KH, ROWS, 2 * D), BF),
            V((KH, ROWS, D), BF),
            V((KH, ROWS, 2 * D), BF),
            V((2, CACHE, NK * D), BF),
            V((2, CACHE, NK * D), BF),
            V((ROWS, KH * G * D), BF),
            V((KH * G, ROWS, D), F32),
            V((KH * G, ROWS, D), F32),
            V((KH * G, ROWS, D), F32),
            V((KH * G, ROWS, D), F32),
            V((NK * G, D), F32),
            V((NK * G * 4, D), F32),
            V((2, NK, 32, D), F32),
            V((16, NK * D), F32),
            V((2, D, NK * D), BF),
            V((2, D, NK * D), BF),
            V((2, NK, 32, D), F32),
            V((OWN, B1, D), BF),
            V((2 * OWN, B1, D), BF),
            V((B2, D), F32),
            V((YS, B2, D), F32),
            V((OWN, 2 * B2, D), F32),
            V((OWN, 2 * B2, D), F32),
            V((B4, D), BF),
            V((HEADS, B4, D), BF),
            V((KH, D, D), F32),
            V((8, D), F32),
            DMA((7,)), DMA((KH,)), DMA((4,)), DMA((4,)),
            DMA((2 * OWN,)), DMA((2 * OWN,)), DMA((YS,)), DMA((YS,)),
            DMA((OWN,)), DMA((OWN,)), DMA((HEADS,)), DMA((HEADS,)),
        ],
        compiler_params=pltpu.CompilerParams(
            collective_id=0, has_side_effects=True, vmem_limit_bytes=60 * 2**20
        ),
    )(
        queries, keys, values, memory_init, norm_init, gate_logits.reshape(1, -1),
        dec_queries, cache_keys, cache_values, new_keys, new_values, cache_lengths,
    )


def solution(mesh):
    rows = ("seq", "grp")
    every = ("seq", "head", "grp")
    in_specs = (
        P(rows, "head"),
        P(rows, "head"),
        P(rows, "head"),
        P("head", None, None),
        P("head", None),
        P(),
        P(every, None, None),
        P(every, None, None),
        P(every, None, None),
        P(every, None, None),
        P(every, None, None),
        P(every),
    )
    out_specs = (P(rows, "head"), P(every, None, None))
    return jax.shard_map(
        on_device, mesh=mesh, in_specs=in_specs, out_specs=out_specs, check_vma=False
    )
```

```python
import functools
import math

import jax
import jax.numpy as jnp
from jax import lax
from jax.experimental import pallas as pl
from jax.experimental.pallas import tpu as pltpu
from jax.sharding import PartitionSpec as P

MESH = pl.DeviceIdType.MESH
BF = jnp.bfloat16
F32 = jnp.float32

D = 128
ROWS = 512
G = 8
KH = 2
NK = 8
STEPS = 3
CACHE = 512
OWN = 8
YS = 4
HEADS = 4
SL = D // OWN
B2 = KH * SL + 8
B4 = KH * D + 16
CHUNKS = 2
CH = ROWS // CHUNKS
AHEAD = 2
UNROLL = 8
LOG2E = 1.4426950408889634
C = LOG2E / math.sqrt(D)
NEG = -1e30


def dot(a, b):
    return lax.dot_general(a, b, (((1,), (0,)), ((), ())), preferred_element_type=F32)


def dot_nt(a, b):
    return lax.dot_general(a, b, (((1,), (1,)), ((), ())), preferred_element_type=F32)


def dot_tn(a, b):
    return lax.dot_general(a, b, (((0,), (0,)), ((), ())), preferred_element_type=F32)


def lift(x):
    return jnp.where(x > 0, x + 1.0, jnp.exp(jnp.minimum(x, 0.0)))


def split(x):
    hi = x.astype(BF)
    return hi, (x - hi.astype(F32)).astype(BF)


def inverse(x):
    r = pl.reciprocal(x, approx=True)
    r = r * (2.0 - x * r)
    return r * (2.0 - x * r)


def lanes(s):
    return [s[:, i * D : (i + 1) * D] for i in range(s.shape[1] // D)]


def row_max(tiles):
    top = functools.reduce(jnp.maximum, tiles)
    return jnp.broadcast_to(jnp.max(top, axis=1, keepdims=True), top.shape)


def weights_of(tiles, top):
    shift = top * C
    return jnp.concatenate([jnp.exp2(t * C - shift).astype(BF) for t in tiles], axis=1)


def each(count, unroll, body):
    def some(i, carry):
        for u in range(unroll):
            body(i * unroll + u)
        return carry

    if count == unroll:
        some(0, 0)
    else:
        lax.fori_loop(0, count // unroll, some, 0)


def kernel(
    q_hbm, k_hbm, v_hbm, mem_init, norm_init, gates, dq, ck_hbm, cv_hbm, nk, nv, lengths,
    out_hbm, dec_out,
    q, kv, kve, ck, cv, out,
    acc, den, top, ret,
    gm, gd, qd, nf, fk, fv, dloc,
    pf, snd0, r0, snd1, r1, snd2, r2, snd3, r3, snd4, r4, r5, prior, pnorm,
    lsem, osem, kvs, kvr, s0, rs0, s1, rs1, s2, rs2, s3, rs3, s4, rs4, s5, rs5,
):
    seq = lax.axis_index("seq")
    head = lax.axis_index("head")
    grp = lax.axis_index("grp")
    y = seq // OWN
    o = seq % OWN

    loads = []
    for j in range(KH):
        cols = pl.ds(j * D, D)
        loads.append(pltpu.make_async_copy(k_hbm.at[:, cols], kv.at[j, :, 0:D], lsem.at[j]))
        loads.append(
            pltpu.make_async_copy(v_hbm.at[:, cols], kv.at[j, :, D : 2 * D], lsem.at[KH + j])
        )
    load_q = pltpu.make_async_copy(q_hbm, q, lsem.at[4])
    load_ck = pltpu.make_async_copy(ck_hbm, ck, lsem.at[5])
    load_cv = pltpu.make_async_copy(cv_hbm, cv, lsem.at[6])
    for copy in loads:
        copy.start()
    load_q.start()
    load_ck.start()
    load_cv.start()

    def grp_peer():
        return {"grp": 1 - grp}

    def row_peer(n):
        return {"seq": y * OWN + (o + n) % OWN}

    def y_peer(n):
        return {"seq": ((y + n) % YS) * OWN + o}

    def head_peer(n):
        return {"head": (head + n) % HEADS}

    peers = [grp_peer()]
    peers += [row_peer(n) for n in range(1, OWN)]
    peers += [y_peer(n) for n in range(1, YS)]
    peers += [head_peer(n) for n in range(1, HEADS)]
    barrier = pltpu.get_barrier_semaphore()
    for peer in peers:
        pl.semaphore_signal(barrier, inc=1, device_id=peer, device_id_type=MESH)

    for j in range(KH):
        kv[j, :, 2 * D :] = jnp.ones((ROWS, D), BF)
        kve[j, :, 2 * D :] = jnp.ones((ROWS, D), BF)
    for copy in loads:
        copy.wait()

    row16 = lax.broadcasted_iota(jnp.int32, (16, D), 0)
    norm_rows = jnp.zeros((16, D), F32)
    for j in range(KH):
        lifted = lift(kv[j, :, 0:D].astype(F32)).astype(BF)
        pf[j * D : (j + 1) * D, :] = dot_tn(lifted, kv[j, :, D : 2 * D])
        norm_rows = norm_rows + jnp.where(
            row16 == j, dot(jnp.ones((16, ROWS), BF), lifted), 0.0
        )
    pf[KH * D :, :] = norm_rows
    snd0[...] = pf[...].astype(BF)

    pl.semaphore_wait(barrier, len(peers))

    def copy0():
        return pltpu.make_async_remote_copy(
            snd0, r0, s0.at[0], rs0.at[0], device_id=grp_peer(), device_id_type=MESH
        )

    copy0().start()

    def kv_copy(c):
        j = c // CHUNKS
        rows = pl.ds(c % CHUNKS * CH, CH)
        return pltpu.make_async_remote_copy(
            kv.at[j, rows, 0 : 2 * D], kve.at[j, rows, 0 : 2 * D], kvs.at[c], kvr.at[c],
            device_id=grp_peer(), device_id_type=MESH,
        )

    def pump(c):
        if c < KH * CHUNKS:

            @pl.when(grp == 0)
            def _():
                kv_copy(c - AHEAD).wait_send()
                kv_copy(c).start()

    def kv_arrived(j, first, last):
        for c in range(j * CHUNKS + first // CH, j * CHUNKS + last // CH):
            kv_copy(c).wait_recv()

    logits = gates[...]
    sig = 1.0 / (1.0 + jnp.exp(-logits))
    at = lax.broadcasted_iota(jnp.int32, (NK * G, NK * G), 0)
    col = lax.broadcasted_iota(jnp.int32, (NK * G, NK * G), 1)
    gm[...] = jnp.broadcast_to(
        jnp.sum(jnp.where(at == col, sig, 0.0), axis=1, keepdims=True), (NK * G, D)
    )
    at = lax.broadcasted_iota(jnp.int32, (NK * G * 4, NK * G), 0)
    col = lax.broadcasted_iota(jnp.int32, (NK * G * 4, NK * G), 1)
    own_row = (at >= col * 4) & (at < col * 4 + 4)
    gd[...] = jnp.broadcast_to(
        jnp.sum(jnp.where(own_row, sig, 0.0), axis=1, keepdims=True), (NK * G * 4, D)
    )

    load_q.wait()

    half = ROWS // 2
    halves = [pl.ds(b * half, half) for b in range(2)]
    r_at = lax.broadcasted_iota(jnp.int32, (half, D), 0)
    c_at = lax.broadcasted_iota(jnp.int32, (half, D), 1)

    def head_lane(h):
        return pl.ds(h * D if isinstance(h, int) else pl.multiple_of(h * D, D), D)

    def own_rows(j):
        def one(gi):
            h = j * G + gi
            queries = [q[rows, head_lane(h)] for rows in halves]
            results = []
            for b in range(2):
                seen = pl.ds(0, (b + 1) * half)
                tiles = lanes(dot_nt(queries[b], kv[j, seen, 0:D]))
                n = len(tiles)
                for i in range(2):
                    tiles[n - 2 + i] = jnp.where(c_at + i * D <= r_at, tiles[n - 2 + i], NEG)
                m = row_max(tiles)
                results.append((m, dot(weights_of(tiles, m), kv[j, seen, D:])))
            for rows, (m, res) in zip(halves, results):
                acc[h, rows, :] = res[:, :D]
                den[h, rows, :] = res[:, D:]
                top[h, rows, :] = m

        each(G, UNROLL, one)

    def square(j, first, last, store):
        seen = pl.ds(first, last - first)

        def one(gi):
            h = j * G + gi
            queries = [q[rows, head_lane(h)] for rows in halves]
            tops = [top[h, rows, :] for rows in halves]
            results = []
            for b in range(2):
                tiles = lanes(dot_nt(queries[b], kve[j, seen, 0:D]))
                m = jnp.maximum(row_max(tiles), tops[b])
                res = dot(weights_of(tiles, m), kve[j, seen, D:])
                fade = jnp.exp2((tops[b] - m) * C)
                results.append((m, fade, res))
            results = [
                (m, acc[h, rows, :] * fade + res[:, :D], den[h, rows, :] * fade + res[:, D:])
                for rows, (m, fade, res) in zip(halves, results)
            ]
            store(h, results)

        each(G, UNROLL, one)

    def keep(h, results):
        for rows, (m, numer, denom) in zip(halves, results):
            acc[h, rows, :] = numer
            den[h, rows, :] = denom
            top[h, rows, :] = m

    def gate_of(h):
        return gm[pl.ds(head * KH * G + h, 1), :]

    def finish(h, results):
        gate = gate_of(h)
        parts = [ret[h, rows, :] for rows in halves]
        for rows, part, (m, numer, denom) in zip(halves, parts, results):
            out[rows, head_lane(h)] = (part + (1.0 - gate) * numer * inverse(denom)).astype(BF)

    own_rows(0)

    copy0().wait_send()

    @pl.when(grp == 0)
    def _():
        for c in range(AHEAD):
            kv_copy(c).start()


    copy0().wait_recv()
    for t in range(OWN):
        for j in range(KH):
            rows = pl.ds(j * D + t * SL, SL)
            snd1[t, j * SL : (j + 1) * SL, :] = pf[rows, :] + r0[rows, :].astype(F32)
        snd1[t, KH * SL :, :] = (pf[KH * D :, :] + r0[KH * D :, :].astype(F32))[0:8]
    r1[o] = snd1[o]

    def send1(n):
        return pltpu.make_async_remote_copy(
            snd1.at[(o + n) % OWN], r1.at[o], s1.at[n], rs1.at[n], device_id=row_peer(n), device_id_type=MESH
        )

    def recv1(n):
        return pltpu.make_async_remote_copy(
            snd1.at[o], r1.at[(o + OWN - n) % OWN], s1.at[n], rs1.at[n],
            device_id=row_peer(n), device_id_type=MESH,
        )

    for n in range(1, OWN):
        send1(n).start()

    own_rows(1)

    for n in range(1, OWN):
        recv1(n).wait_recv()
    run = jnp.zeros((B2, D), F32)
    for t in range(OWN):
        snd3[t] = run[0 : KH * SL]
        run = run + r1[t]
    snd2[...] = run
    r2[y] = run

    def send2(n):
        return pltpu.make_async_remote_copy(
            snd2, r2.at[y], s2.at[n], rs2.at[n], device_id=y_peer(n), device_id_type=MESH
        )

    def recv2(n):
        return pltpu.make_async_remote_copy(
            snd2, r2.at[(y + YS - n) % YS], s2.at[n], rs2.at[n], device_id=y_peer(n), device_id_type=MESH
        )

    for n in range(1, YS):
        send2(n).start()

    qd[...] = jnp.zeros_like(qd)
    fk[...] = jnp.zeros_like(fk)
    fv[...] = jnp.zeros_like(fv)
    nf[...] = jnp.zeros_like(nf)
    for t in range(STEPS):
        for h in range(NK * G):
            j, gi = divmod(h, G)
            two = dq[t, :, h * D : (h + 1) * D].astype(F32)
            for r in range(2):
                qd[j, r * 32 + gi * 4 + t : r * 32 + gi * 4 + t + 1, :] = two[r : r + 1]
    for fresh, wide in ((nk, fk), (nv, fv)):
        for t in range(STEPS):
            two = fresh[t].astype(F32)
            for r in range(2):
                nf[r, t : t + 1, :] = two[r : r + 1]
        for r in range(2):
            wide[r, 0:16, :] = nf[r].astype(BF)
    load_ck.wait()
    load_cv.wait()

    c64 = lax.broadcasted_iota(jnp.int32, (64, D), 1)
    t64 = lax.broadcasted_iota(jnp.int32, (64, D), 0) % 4
    fresh_ok = (c64 <= t64) & (c64 < STEPS)

    def decode(r):
        length = lengths[r]

        def one(p):
            lane = pl.ds(p * 2 * D, 2 * D)
            none = jnp.zeros((32, D), BF)
            q0 = qd[2 * p, 32 * r : 32 * r + 32, :].astype(BF)
            q1 = qd[2 * p + 1, 32 * r : 32 * r + 32, :].astype(BF)
            both = jnp.concatenate(
                [jnp.concatenate([q0, none], axis=1), jnp.concatenate([none, q1], axis=1)], axis=0
            )
            tiles = lanes(dot_nt(both, ck[r, :, lane]))
            tiles = [jnp.where(c64 + i * D < length, s, NEG) for i, s in enumerate(tiles)]
            tiles.append(jnp.where(fresh_ok, dot_nt(both, fk[r, :, lane]), NEG))
            shift = row_max(tiles) * C
            ws = [jnp.exp2(s * C - shift) for s in tiles]
            tot = jnp.sum(functools.reduce(jnp.add, ws), axis=1, keepdims=True)
            ws = [w.astype(BF) for w in ws]
            res = dot(jnp.concatenate(ws[:-1], axis=1), cv[r, :, lane]) + dot(ws[-1], fv[r, :, lane])
            res = res / tot
            dloc[2 * p, 32 * r : 32 * r + 32, :] = res[0:32, 0:D]
            dloc[2 * p + 1, 32 * r : 32 * r + 32, :] = res[32:64, D:]

        each(NK // 2, NK // 2, one)

    decode(0)
    pump(AHEAD)

    for n in range(1, YS):
        recv2(n).wait_recv()
    base = jnp.zeros((B2, D), F32)
    total = jnp.zeros((B2, D), F32)
    for t in range(YS):
        base = base + jnp.where(t < y, r2[t], 0.0)
        total = total + r2[t]
    for t in range(OWN):
        snd3[t] = snd3[t] + base[0 : KH * SL]
    r3[o] = snd3[o]

    def send3(n):
        return pltpu.make_async_remote_copy(
            snd3.at[(o + n) % OWN], r3.at[o], s3.at[n], rs3.at[n], device_id=row_peer(n), device_id_type=MESH
        )

    def recv3(n):
        return pltpu.make_async_remote_copy(
            snd3.at[o], r3.at[(o + OWN - n) % OWN], s3.at[n], rs3.at[n],
            device_id=row_peer(n), device_id_type=MESH,
        )

    for n in range(1, OWN):
        send3(n).start()

    row8 = lax.broadcasted_iota(jnp.int32, (8, D), 0)
    init8 = jnp.zeros((8, D), F32)
    for j in range(KH):
        init8 = init8 + jnp.where(row8 == j, norm_init[j : j + 1, :], 0.0)
    before = base[KH * SL :] + init8
    for t in range(OWN):
        before = before + jnp.where(t < o, r1[t, KH * SL :, :], 0.0)
    pnorm[...] = before
    for j in range(KH):
        init = mem_init[j, pl.ds(pl.multiple_of(o * SL, SL), SL), :]
        snd4[j * SL : (j + 1) * SL, :] = (total[j * SL : (j + 1) * SL] + init).astype(BF)
    snd4[KH * SL :, :] = jnp.concatenate(
        [total[KH * SL :] + init8, jnp.zeros((8, D), F32)], axis=0
    ).astype(BF)
    r4[head] = snd4[...]

    def send4(n):
        return pltpu.make_async_remote_copy(
            snd4, r4.at[head], s4.at[n], rs4.at[n], device_id=head_peer(n), device_id_type=MESH
        )

    def recv4(n):
        return pltpu.make_async_remote_copy(
            snd4, r4.at[(head + HEADS - n) % HEADS], s4.at[n], rs4.at[n],
            device_id=head_peer(n), device_id_type=MESH,
        )

    for n in range(1, HEADS):
        send4(n).start()

    decode(1)
    pump(AHEAD + 1)

    for n in range(1, OWN):
        recv3(n).wait_recv()
    for j in range(KH):
        for t in range(OWN):
            at_d = pl.ds(t * SL, SL)
            prior[j, at_d, :] = r3[t, j * SL : (j + 1) * SL, :] + mem_init[j, at_d, :]

    def retrieve(j, last):
        m_hi, m_lo = split(prior[j])
        wide = jnp.concatenate([m_hi, m_lo], axis=1)
        numer_w = jnp.concatenate([wide, wide], axis=0)
        n_hi, n_lo = split(jnp.broadcast_to(pnorm[j : j + 1, :], (D, D)))
        tall = jnp.concatenate([n_hi, n_lo], axis=0)
        denom_w = jnp.concatenate([tall, tall], axis=1)

        def one(gi):
            h = j * G + gi
            gate = gate_of(h)
            queries = [q[rows, head_lane(h)] for rows in halves]
            if last:
                local = [(acc[h, rows, :], den[h, rows, :]) for rows in halves]
            results = []
            for b in range(2):
                hi, lo = split(lift(queries[b].astype(F32)))
                pair = jnp.concatenate([hi, lo], axis=1)
                numer = dot(pair, numer_w)
                denom = dot_nt(pair, denom_w)
                got = (numer[:, :D] + numer[:, D:]) * inverse(denom[:, :D] + denom[:, D:]) * gate
                if last:
                    got = got + (1.0 - gate) * local[b][0] * inverse(local[b][1])
                results.append(got)
            for rows, got in zip(halves, results):
                if last:
                    out[rows, head_lane(h)] = got.astype(BF)
                else:
                    ret[h, rows, :] = got

        each(G, UNROLL, one)

    def out_copy(j):
        cols = pl.ds(j * G * D, G * D)
        return pltpu.make_async_copy(out.at[:, cols], out_hbm.at[:, cols], osem.at[j])

    @pl.when(grp == 0)
    def _():
        for j in range(KH):
            retrieve(j, True)
            out_copy(j).start()

    @pl.when(grp == 1)
    def _():
        for j in range(KH):
            retrieve(j, False)

    for n in range(1, HEADS):
        recv4(n).wait_recv()
    r5[o] = r4[:, 0 : KH * SL, :]

    def send5(n):
        return pltpu.make_async_remote_copy(
            r4.at[:, 0 : KH * SL, :], r5.at[o], s5.at[n], rs5.at[n],
            device_id=row_peer(n), device_id_type=MESH,
        )

    def recv5(n):
        return pltpu.make_async_remote_copy(
            r4.at[:, 0 : KH * SL, :], r5.at[(o + OWN - n) % OWN], s5.at[n], rs5.at[n],
            device_id=row_peer(n), device_id_type=MESH,
        )

    for n in range(1, OWN):
        send5(n).start()


    @pl.when(grp == 1)
    def _():
        kv_arrived(0, 0, ROWS)
        square(0, 0, ROWS, finish)
        out_copy(0).start()
        kv_arrived(1, 0, half)
        square(1, 0, half, keep)

    for n in range(1, OWN):
        recv5(n).wait_recv()
    for j in range(NK):
        at_s = (j % KH) * SL
        m_one = jnp.concatenate([r5[t, j // KH, at_s : at_s + SL, :] for t in range(OWN)], axis=0)
        numer_w = jnp.concatenate([m_one, m_one], axis=0)
        n_rows = r4[j // KH, KH * SL :, :].astype(F32)
        n_one = jnp.broadcast_to(n_rows[j % KH : j % KH + 1, :], (D, D)).astype(BF)
        denom_w = jnp.concatenate([n_one, n_one], axis=1)
        hi, lo = split(lift(qd[j]))
        pair = jnp.concatenate([hi, lo], axis=1)
        got = dot(pair, numer_w) * inverse(dot_nt(pair, denom_w))
        gate = gd[j * G * 4 : (j + 1) * G * 4, :]
        gate = jnp.concatenate([gate, gate], axis=0)
        mixed = gate * got + (1.0 - gate) * dloc[j]
        for gi in range(G):
            at_h = (j * G + gi) * D
            for t in range(STEPS):
                row = gi * 4 + t
                dec_out[t, :, at_h : at_h + D] = jnp.concatenate(
                    [mixed[row : row + 1], mixed[32 + row : 33 + row]], axis=0
                ).astype(BF)

    @pl.when(grp == 1)
    def _():
        kv_arrived(1, half, ROWS)
        square(1, half, ROWS, finish)
        out_copy(1).start()

    @pl.when(grp == 0)
    def _():
        for c in range(KH * CHUNKS - AHEAD, KH * CHUNKS):
            kv_copy(c).wait_send()

    for n in range(1, OWN):
        send1(n).wait_send()
    for n in range(1, YS):
        send2(n).wait_send()
    for n in range(1, OWN):
        send3(n).wait_send()
    for n in range(1, HEADS):
        send4(n).wait_send()
    for n in range(1, OWN):
        send5(n).wait_send()
    for j in range(KH):
        out_copy(j).wait()


def on_device(
    queries, keys, values, memory_init, norm_init, gate_logits,
    dec_queries, cache_keys, cache_values, new_keys, new_values, cache_lengths,
):
    hbm = pl.BlockSpec(memory_space=pl.ANY)
    vmem = pl.BlockSpec(memory_space=pltpu.VMEM)
    smem = pl.BlockSpec(memory_space=pltpu.SMEM)
    V = pltpu.VMEM
    DMA = pltpu.SemaphoreType.DMA
    prefill, decoded = pl.pallas_call(
        kernel,
        out_shape=(
            jax.ShapeDtypeStruct((ROWS, KH * G * D), BF),
            jax.ShapeDtypeStruct((STEPS, 2, NK * G * D), BF),
        ),
        in_specs=[hbm, hbm, hbm, vmem, vmem, vmem, vmem, hbm, hbm, vmem, vmem, smem],
        out_specs=(hbm, vmem),
        scratch_shapes=[
            V((ROWS, KH * G * D), BF),
            V((KH, ROWS, 3 * D), BF),
            V((KH, ROWS, 3 * D), BF),
            V((2, CACHE, NK * D), BF),
            V((2, CACHE, NK * D), BF),
            V((ROWS, KH * G * D), BF),
            V((KH * G, ROWS, D), F32),
            V((KH * G, ROWS, D), F32),
            V((KH * G, ROWS, D), F32),
            V((KH * G, ROWS, D), F32),
            V((NK * G, D), F32),
            V((NK * G * 4, D), F32),
            V((NK, 64, D), F32),
            V((2, 16, NK * D), F32),
            V((2, D, NK * D), BF),
            V((2, D, NK * D), BF),
            V((NK, 64, D), F32),
            V((B4, D), F32),
            V((B4, D), BF),
            V((B4, D), BF),
            V((OWN, B2, D), F32),
            V((OWN, B2, D), F32),
            V((B2, D), F32),
            V((YS, B2, D), F32),
            V((OWN, KH * SL, D), F32),
            V((OWN, KH * SL, D), F32),
            V((KH * SL + 16, D), BF),
            V((HEADS, KH * SL + 16, D), BF),
            V((OWN, HEADS, KH * SL, D), BF),
            V((KH, D, D), F32),
            V((8, D), F32),
            DMA((7,)), DMA((KH,)), DMA((KH * CHUNKS,)), DMA((KH * CHUNKS,)), DMA((1,)), DMA((1,)),
            DMA((OWN,)), DMA((OWN,)), DMA((YS,)), DMA((YS,)),
            DMA((OWN,)), DMA((OWN,)), DMA((HEADS,)), DMA((HEADS,)),
            DMA((OWN,)), DMA((OWN,)),
        ],
        compiler_params=pltpu.CompilerParams(
            collective_id=0, has_side_effects=True, vmem_limit_bytes=60 * 2**20
        ),
    )(
        queries, keys, values, memory_init, norm_init, gate_logits.reshape(1, -1),
        dec_queries.transpose(1, 0, 2), cache_keys, cache_values,
        new_keys.transpose(1, 0, 2), new_values.transpose(1, 0, 2), cache_lengths,
    )
    return prefill, decoded.transpose(1, 0, 2)


def solution(mesh):
    rows = ("seq", "grp")
    every = ("seq", "head", "grp")
    in_specs = (
        P(rows, "head"),
        P(rows, "head"),
        P(rows, "head"),
        P("head", None, None),
        P("head", None),
        P(),
        P(every, None, None),
        P(every, None, None),
        P(every, None, None),
        P(every, None, None),
        P(every, None, None),
        P(every),
    )
    out_specs = (P(rows, "head"), P(every, None, None))
    return jax.shard_map(
        on_device, mesh=mesh, in_specs=in_specs, out_specs=out_specs, check_vma=False
    )
```

```python
import functools
import math

import jax
import jax.numpy as jnp
from jax import lax
from jax.experimental import pallas as pl
from jax.experimental.pallas import tpu as pltpu
from jax.sharding import PartitionSpec as P

MESH = pl.DeviceIdType.MESH
BF = jnp.bfloat16
F32 = jnp.float32

D = 128
ROWS = 512
G = 8
KH = 2
NK = 8
STEPS = 3
CACHE = 512
OWN = 8
YS = 4
HEADS = 4
SL = D // OWN
B2 = KH * SL + 8
B4 = KH * D + 16
CHUNKS = 2
CH = ROWS // CHUNKS
AHEAD = 2
UNROLL = 8
LOG2E = 1.4426950408889634
C = LOG2E / math.sqrt(D)
NEG = -1e30


def dot(a, b):
    return lax.dot_general(a, b, (((1,), (0,)), ((), ())), preferred_element_type=F32)


def dot_nt(a, b):
    return lax.dot_general(a, b, (((1,), (1,)), ((), ())), preferred_element_type=F32)


def dot_tn(a, b):
    return lax.dot_general(a, b, (((0,), (0,)), ((), ())), preferred_element_type=F32)


def lift(x):
    return jnp.where(x > 0, x + 1.0, jnp.exp(jnp.minimum(x, 0.0)))


def split(x):
    hi = x.astype(BF)
    return hi, (x - hi.astype(F32)).astype(BF)


def inverse(x):
    r = pl.reciprocal(x, approx=True)
    r = r * (2.0 - x * r)
    return r * (2.0 - x * r)


def lanes(s):
    return [s[:, i * D : (i + 1) * D] for i in range(s.shape[1] // D)]


def row_max(tiles):
    top = functools.reduce(jnp.maximum, tiles)
    return jnp.broadcast_to(jnp.max(top, axis=1, keepdims=True), top.shape)


def weights_of(tiles, top):
    shift = top * C
    return jnp.concatenate([jnp.exp2(t * C - shift).astype(BF) for t in tiles], axis=1)


def each(count, unroll, body):
    def some(i, carry):
        for u in range(unroll):
            body(i * unroll + u)
        return carry

    if count == unroll:
        some(0, 0)
    else:
        lax.fori_loop(0, count // unroll, some, 0)


def kernel(
    q_hbm, k_hbm, v_hbm, mem_init, norm_init, gates, dq, ck_hbm, cv_hbm, nk, nv, lengths,
    out, dec_out,
    q, kv, kve, ck, cv,
    acc, den, top, ret,
    gm, gd, qd, nf, fk, fv, dloc,
    pf, snd0, r0, snd1, r1, snd2, r2, snd3, r3, snd4, r4, r5, prior, pnorm,
    lsem, kvs, kvr, s0, rs0, s1, rs1, s2, rs2, s3, rs3, s4, rs4, s5, rs5,
):
    seq = lax.axis_index("seq")
    head = lax.axis_index("head")
    grp = lax.axis_index("grp")
    y = seq // OWN
    o = seq % OWN

    loads = []
    for j in range(KH):
        cols = pl.ds(j * D, D)
        loads.append(pltpu.make_async_copy(k_hbm.at[:, cols], kv.at[j, :, 0:D], lsem.at[j]))
        loads.append(
            pltpu.make_async_copy(v_hbm.at[:, cols], kv.at[j, :, D : 2 * D], lsem.at[KH + j])
        )
    load_q = pltpu.make_async_copy(q_hbm, q, lsem.at[4])
    load_ck = pltpu.make_async_copy(ck_hbm, ck, lsem.at[5])
    load_cv = pltpu.make_async_copy(cv_hbm, cv, lsem.at[6])
    for copy in loads:
        copy.start()
    load_q.start()
    load_ck.start()
    load_cv.start()

    def grp_peer():
        return {"grp": 1 - grp}

    def row_peer(n):
        return {"seq": y * OWN + (o + n) % OWN}

    def y_peer(n):
        return {"seq": ((y + n) % YS) * OWN + o}

    def head_peer(n):
        return {"head": (head + n) % HEADS}

    peers = [grp_peer()]
    peers += [row_peer(n) for n in range(1, OWN)]
    peers += [y_peer(n) for n in range(1, YS)]
    peers += [head_peer(n) for n in range(1, HEADS)]
    barrier = pltpu.get_barrier_semaphore()
    for peer in peers:
        pl.semaphore_signal(barrier, inc=1, device_id=peer, device_id_type=MESH)

    for j in range(KH):
        kv[j, :, 2 * D :] = jnp.ones((ROWS, D), BF)
        kve[j, :, 2 * D :] = jnp.ones((ROWS, D), BF)
    for copy in loads:
        copy.wait()

    row16 = lax.broadcasted_iota(jnp.int32, (16, D), 0)
    norm_rows = jnp.zeros((16, D), F32)
    for j in range(KH):
        lifted = lift(kv[j, :, 0:D].astype(F32)).astype(BF)
        pf[j * D : (j + 1) * D, :] = dot_tn(lifted, kv[j, :, D : 2 * D])
        norm_rows = norm_rows + jnp.where(
            row16 == j, dot(jnp.ones((16, ROWS), BF), lifted), 0.0
        )
    pf[KH * D :, :] = norm_rows
    snd0[...] = pf[...].astype(BF)

    pl.semaphore_wait(barrier, len(peers))

    def copy0():
        return pltpu.make_async_remote_copy(
            snd0, r0, s0.at[0], rs0.at[0], device_id=grp_peer(), device_id_type=MESH
        )

    copy0().start()

    def kv_copy(c):
        j = c // CHUNKS
        rows = pl.ds(c % CHUNKS * CH, CH)
        return pltpu.make_async_remote_copy(
            kv.at[j, rows, 0 : 2 * D], kve.at[j, rows, 0 : 2 * D], kvs.at[c], kvr.at[c],
            device_id=grp_peer(), device_id_type=MESH,
        )

    def pump(c):
        if c < KH * CHUNKS:

            @pl.when(grp == 0)
            def _():
                kv_copy(c - AHEAD).wait_send()
                kv_copy(c).start()

    def kv_arrived(j, first, last):
        for c in range(j * CHUNKS + first // CH, j * CHUNKS + last // CH):
            kv_copy(c).wait_recv()

    logits = gates[...]
    sig = 1.0 / (1.0 + jnp.exp(-logits))
    at = lax.broadcasted_iota(jnp.int32, (NK * G, NK * G), 0)
    col = lax.broadcasted_iota(jnp.int32, (NK * G, NK * G), 1)
    gm[...] = jnp.broadcast_to(
        jnp.sum(jnp.where(at == col, sig, 0.0), axis=1, keepdims=True), (NK * G, D)
    )
    at = lax.broadcasted_iota(jnp.int32, (NK * G * 4, NK * G), 0)
    col = lax.broadcasted_iota(jnp.int32, (NK * G * 4, NK * G), 1)
    own_row = (at >= col * 4) & (at < col * 4 + 4)
    gd[...] = jnp.broadcast_to(
        jnp.sum(jnp.where(own_row, sig, 0.0), axis=1, keepdims=True), (NK * G * 4, D)
    )

    load_q.wait()

    half = ROWS // 2
    halves = [pl.ds(b * half, half) for b in range(2)]
    r_at = lax.broadcasted_iota(jnp.int32, (half, D), 0)
    c_at = lax.broadcasted_iota(jnp.int32, (half, D), 1)

    def head_lane(h):
        return pl.ds(h * D if isinstance(h, int) else pl.multiple_of(h * D, D), D)

    def own_rows(j):
        def one(gi):
            h = j * G + gi
            queries = [q[rows, head_lane(h)] for rows in halves]
            results = []
            for b in range(2):
                seen = pl.ds(0, (b + 1) * half)
                tiles = lanes(dot_nt(queries[b], kv[j, seen, 0:D]))
                n = len(tiles)
                for i in range(2):
                    tiles[n - 2 + i] = jnp.where(c_at + i * D <= r_at, tiles[n - 2 + i], NEG)
                m = row_max(tiles)
                results.append((m, dot(weights_of(tiles, m), kv[j, seen, D:])))
            for rows, (m, res) in zip(halves, results):
                acc[h, rows, :] = res[:, :D]
                den[h, rows, :] = res[:, D:]
                top[h, rows, :] = m

        each(G, UNROLL, one)

    def square(j, first, last, store):
        seen = pl.ds(first, last - first)

        def one(gi):
            h = j * G + gi
            queries = [q[rows, head_lane(h)] for rows in halves]
            tops = [top[h, rows, :] for rows in halves]
            results = []
            for b in range(2):
                tiles = lanes(dot_nt(queries[b], kve[j, seen, 0:D]))
                m = jnp.maximum(row_max(tiles), tops[b])
                res = dot(weights_of(tiles, m), kve[j, seen, D:])
                fade = jnp.exp2((tops[b] - m) * C)
                results.append((m, fade, res))
            results = [
                (m, acc[h, rows, :] * fade + res[:, :D], den[h, rows, :] * fade + res[:, D:])
                for rows, (m, fade, res) in zip(halves, results)
            ]
            store(h, results)

        each(G, UNROLL, one)

    def keep(h, results):
        for rows, (m, numer, denom) in zip(halves, results):
            acc[h, rows, :] = numer
            den[h, rows, :] = denom
            top[h, rows, :] = m

    def gate_of(h):
        return gm[pl.ds(head * KH * G + h, 1), :]

    def finish(h, results):
        gate = gate_of(h)
        parts = [ret[h, rows, :] for rows in halves]
        for rows, part, (m, numer, denom) in zip(halves, parts, results):
            out[rows, head_lane(h)] = (part + (1.0 - gate) * numer * inverse(denom)).astype(BF)

    own_rows(0)

    copy0().wait_send()

    @pl.when(grp == 0)
    def _():
        for c in range(AHEAD):
            kv_copy(c).start()


    copy0().wait_recv()
    for t in range(OWN):
        for j in range(KH):
            rows = pl.ds(j * D + t * SL, SL)
            snd1[t, j * SL : (j + 1) * SL, :] = pf[rows, :] + r0[rows, :].astype(F32)
        snd1[t, KH * SL :, :] = (pf[KH * D :, :] + r0[KH * D :, :].astype(F32))[0:8]
    r1[o] = snd1[o]

    def send1(n):
        return pltpu.make_async_remote_copy(
            snd1.at[(o + n) % OWN], r1.at[o], s1.at[n], rs1.at[n], device_id=row_peer(n), device_id_type=MESH
        )

    def recv1(n):
        return pltpu.make_async_remote_copy(
            snd1.at[o], r1.at[(o + OWN - n) % OWN], s1.at[n], rs1.at[n],
            device_id=row_peer(n), device_id_type=MESH,
        )

    for n in range(1, OWN):
        send1(n).start()

    own_rows(1)

    for n in range(1, OWN):
        recv1(n).wait_recv()
    run = jnp.zeros((B2, D), F32)
    for t in range(OWN):
        snd3[t] = run[0 : KH * SL]
        run = run + r1[t]
    snd2[...] = run
    r2[y] = run

    def send2(n):
        return pltpu.make_async_remote_copy(
            snd2, r2.at[y], s2.at[n], rs2.at[n], device_id=y_peer(n), device_id_type=MESH
        )

    def recv2(n):
        return pltpu.make_async_remote_copy(
            snd2, r2.at[(y + YS - n) % YS], s2.at[n], rs2.at[n], device_id=y_peer(n), device_id_type=MESH
        )

    for n in range(1, YS):
        send2(n).start()

    qd[...] = jnp.zeros_like(qd)
    fk[...] = jnp.zeros_like(fk)
    fv[...] = jnp.zeros_like(fv)
    nf[...] = jnp.zeros_like(nf)
    for t in range(STEPS):
        for h in range(NK * G):
            j, gi = divmod(h, G)
            two = dq[t, :, h * D : (h + 1) * D].astype(F32)
            for r in range(2):
                qd[j, r * 32 + gi * 4 + t : r * 32 + gi * 4 + t + 1, :] = two[r : r + 1]
    for fresh, wide in ((nk, fk), (nv, fv)):
        for t in range(STEPS):
            two = fresh[t].astype(F32)
            for r in range(2):
                nf[r, t : t + 1, :] = two[r : r + 1]
        for r in range(2):
            wide[r, 0:16, :] = nf[r].astype(BF)
    load_ck.wait()
    load_cv.wait()

    c64 = lax.broadcasted_iota(jnp.int32, (64, D), 1)
    t64 = lax.broadcasted_iota(jnp.int32, (64, D), 0) % 4
    fresh_ok = (c64 <= t64) & (c64 < STEPS)

    def decode(r):
        length = lengths[r]

        def one(p):
            lane = pl.ds(p * 2 * D, 2 * D)
            none = jnp.zeros((32, D), BF)
            q0 = qd[2 * p, 32 * r : 32 * r + 32, :].astype(BF)
            q1 = qd[2 * p + 1, 32 * r : 32 * r + 32, :].astype(BF)
            both = jnp.concatenate(
                [jnp.concatenate([q0, none], axis=1), jnp.concatenate([none, q1], axis=1)], axis=0
            )
            tiles = lanes(dot_nt(both, ck[r, :, lane]))
            tiles = [jnp.where(c64 + i * D < length, s, NEG) for i, s in enumerate(tiles)]
            tiles.append(jnp.where(fresh_ok, dot_nt(both, fk[r, :, lane]), NEG))
            shift = row_max(tiles) * C
            ws = [jnp.exp2(s * C - shift) for s in tiles]
            tot = jnp.sum(functools.reduce(jnp.add, ws), axis=1, keepdims=True)
            ws = [w.astype(BF) for w in ws]
            res = dot(jnp.concatenate(ws[:-1], axis=1), cv[r, :, lane]) + dot(ws[-1], fv[r, :, lane])
            res = res / tot
            dloc[2 * p, 32 * r : 32 * r + 32, :] = res[0:32, 0:D]
            dloc[2 * p + 1, 32 * r : 32 * r + 32, :] = res[32:64, D:]

        each(NK // 2, NK // 2, one)

    decode(0)

    for n in range(1, YS):
        recv2(n).wait_recv()
    base = jnp.zeros((B2, D), F32)
    total = jnp.zeros((B2, D), F32)
    for t in range(YS):
        base = base + jnp.where(t < y, r2[t], 0.0)
        total = total + r2[t]
    for t in range(OWN):
        snd3[t] = snd3[t] + base[0 : KH * SL]
    r3[o] = snd3[o]

    def send3(n):
        return pltpu.make_async_remote_copy(
            snd3.at[(o + n) % OWN], r3.at[o], s3.at[n], rs3.at[n], device_id=row_peer(n), device_id_type=MESH
        )

    def recv3(n):
        return pltpu.make_async_remote_copy(
            snd3.at[o], r3.at[(o + OWN - n) % OWN], s3.at[n], rs3.at[n],
            device_id=row_peer(n), device_id_type=MESH,
        )

    for n in range(1, OWN):
        send3(n).start()

    row8 = lax.broadcasted_iota(jnp.int32, (8, D), 0)
    init8 = jnp.zeros((8, D), F32)
    for j in range(KH):
        init8 = init8 + jnp.where(row8 == j, norm_init[j : j + 1, :], 0.0)
    before = base[KH * SL :] + init8
    for t in range(OWN):
        before = before + jnp.where(t < o, r1[t, KH * SL :, :], 0.0)
    pnorm[...] = before
    for j in range(KH):
        init = mem_init[j, pl.ds(pl.multiple_of(o * SL, SL), SL), :]
        snd4[j * SL : (j + 1) * SL, :] = (total[j * SL : (j + 1) * SL] + init).astype(BF)
    snd4[KH * SL :, :] = jnp.concatenate(
        [total[KH * SL :] + init8, jnp.zeros((8, D), F32)], axis=0
    ).astype(BF)
    r4[head] = snd4[...]

    def send4(n):
        return pltpu.make_async_remote_copy(
            snd4, r4.at[head], s4.at[n], rs4.at[n], device_id=head_peer(n), device_id_type=MESH
        )

    def recv4(n):
        return pltpu.make_async_remote_copy(
            snd4, r4.at[(head + HEADS - n) % HEADS], s4.at[n], rs4.at[n],
            device_id=head_peer(n), device_id_type=MESH,
        )

    for n in range(1, HEADS):
        send4(n).start()
    pump(AHEAD)

    decode(1)
    pump(AHEAD + 1)

    for n in range(1, OWN):
        recv3(n).wait_recv()
    for j in range(KH):
        for t in range(OWN):
            at_d = pl.ds(t * SL, SL)
            prior[j, at_d, :] = r3[t, j * SL : (j + 1) * SL, :] + mem_init[j, at_d, :]

    def retrieve(j, last):
        m_hi, m_lo = split(prior[j])
        wide = jnp.concatenate([m_hi, m_lo], axis=1)
        numer_w = jnp.concatenate([wide, wide], axis=0)
        n_hi, n_lo = split(jnp.broadcast_to(pnorm[j : j + 1, :], (D, D)))
        tall = jnp.concatenate([n_hi, n_lo], axis=0)
        denom_w = jnp.concatenate([tall, tall], axis=1)

        def one(gi):
            h = j * G + gi
            gate = gate_of(h)
            queries = [q[rows, head_lane(h)] for rows in halves]
            if last:
                local = [(acc[h, rows, :], den[h, rows, :]) for rows in halves]
            results = []
            for b in range(2):
                hi, lo = split(lift(queries[b].astype(F32)))
                pair = jnp.concatenate([hi, lo], axis=1)
                numer = dot(pair, numer_w)
                denom = dot_nt(pair, denom_w)
                got = (numer[:, :D] + numer[:, D:]) * inverse(denom[:, :D] + denom[:, D:]) * gate
                if last:
                    got = got + (1.0 - gate) * local[b][0] * inverse(local[b][1])
                results.append(got)
            for rows, got in zip(halves, results):
                if last:
                    out[rows, head_lane(h)] = got.astype(BF)
                else:
                    ret[h, rows, :] = got

        each(G, UNROLL, one)

    @pl.when(grp == 0)
    def _():
        for j in range(KH):
            retrieve(j, True)

    @pl.when(grp == 1)
    def _():
        for j in range(KH):
            retrieve(j, False)

    for n in range(1, HEADS):
        recv4(n).wait_recv()
    r5[o] = r4[:, 0 : KH * SL, :]

    def send5(n):
        return pltpu.make_async_remote_copy(
            r4.at[:, 0 : KH * SL, :], r5.at[o], s5.at[n], rs5.at[n],
            device_id=row_peer(n), device_id_type=MESH,
        )

    def recv5(n):
        return pltpu.make_async_remote_copy(
            r4.at[:, 0 : KH * SL, :], r5.at[(o + OWN - n) % OWN], s5.at[n], rs5.at[n],
            device_id=row_peer(n), device_id_type=MESH,
        )

    for n in range(1, OWN):
        send5(n).start()


    @pl.when(grp == 1)
    def _():
        kv_arrived(0, 0, ROWS)
        square(0, 0, ROWS, finish)
        kv_arrived(1, 0, half)
        square(1, 0, half, keep)

    for n in range(1, OWN):
        recv5(n).wait_recv()
    for j in range(NK):
        at_s = (j % KH) * SL
        m_one = jnp.concatenate([r5[t, j // KH, at_s : at_s + SL, :] for t in range(OWN)], axis=0)
        numer_w = jnp.concatenate([m_one, m_one], axis=0)
        n_rows = r4[j // KH, KH * SL :, :].astype(F32)
        n_one = jnp.broadcast_to(n_rows[j % KH : j % KH + 1, :], (D, D)).astype(BF)
        denom_w = jnp.concatenate([n_one, n_one], axis=1)
        hi, lo = split(lift(qd[j]))
        pair = jnp.concatenate([hi, lo], axis=1)
        got = dot(pair, numer_w) * inverse(dot_nt(pair, denom_w))
        gate = gd[j * G * 4 : (j + 1) * G * 4, :]
        gate = jnp.concatenate([gate, gate], axis=0)
        mixed = gate * got + (1.0 - gate) * dloc[j]
        for gi in range(G):
            at_h = (j * G + gi) * D
            for t in range(STEPS):
                row = gi * 4 + t
                dec_out[t, :, at_h : at_h + D] = jnp.concatenate(
                    [mixed[row : row + 1], mixed[32 + row : 33 + row]], axis=0
                ).astype(BF)

    @pl.when(grp == 1)
    def _():
        kv_arrived(1, half, ROWS)
        square(1, half, ROWS, finish)

    @pl.when(grp == 0)
    def _():
        for c in range(KH * CHUNKS - AHEAD, KH * CHUNKS):
            kv_copy(c).wait_send()

    for n in range(1, OWN):
        send1(n).wait_send()
    for n in range(1, YS):
        send2(n).wait_send()
    for n in range(1, OWN):
        send3(n).wait_send()
    for n in range(1, HEADS):
        send4(n).wait_send()
    for n in range(1, OWN):
        send5(n).wait_send()


def on_device(
    queries, keys, values, memory_init, norm_init, gate_logits,
    dec_queries, cache_keys, cache_values, new_keys, new_values, cache_lengths,
):
    hbm = pl.BlockSpec(memory_space=pltpu.HBM)
    vmem = pl.BlockSpec(memory_space=pltpu.VMEM)
    smem = pl.BlockSpec(memory_space=pltpu.SMEM)
    V = pltpu.VMEM
    DMA = pltpu.SemaphoreType.DMA
    prefill, decoded = pl.pallas_call(
        kernel,
        out_shape=(
            V((ROWS, KH * G * D), BF),
            V((STEPS, 2, NK * G * D), BF),
        ),
        in_specs=[hbm, hbm, hbm, vmem, vmem, vmem, vmem, hbm, hbm, vmem, vmem, smem],
        out_specs=(vmem, vmem),
        scratch_shapes=[
            V((ROWS, KH * G * D), BF),
            V((KH, ROWS, 3 * D), BF),
            V((KH, ROWS, 3 * D), BF),
            V((2, CACHE, NK * D), BF),
            V((2, CACHE, NK * D), BF),
            V((KH * G, ROWS, D), F32),
            V((KH * G, ROWS, D), F32),
            V((KH * G, ROWS, D), F32),
            V((KH * G, ROWS, D), F32),
            V((NK * G, D), F32),
            V((NK * G * 4, D), F32),
            V((NK, 64, D), F32),
            V((2, 16, NK * D), F32),
            V((2, D, NK * D), BF),
            V((2, D, NK * D), BF),
            V((NK, 64, D), F32),
            V((B4, D), F32),
            V((B4, D), BF),
            V((B4, D), BF),
            V((OWN, B2, D), F32),
            V((OWN, B2, D), F32),
            V((B2, D), F32),
            V((YS, B2, D), F32),
            V((OWN, KH * SL, D), F32),
            V((OWN, KH * SL, D), F32),
            V((KH * SL + 16, D), BF),
            V((HEADS, KH * SL + 16, D), BF),
            V((OWN, HEADS, KH * SL, D), BF),
            V((KH, D, D), F32),
            V((8, D), F32),
            DMA((7,)), DMA((KH * CHUNKS,)), DMA((KH * CHUNKS,)), DMA((1,)), DMA((1,)),
            DMA((OWN,)), DMA((OWN,)), DMA((YS,)), DMA((YS,)),
            DMA((OWN,)), DMA((OWN,)), DMA((HEADS,)), DMA((HEADS,)),
            DMA((OWN,)), DMA((OWN,)),
        ],
        compiler_params=pltpu.CompilerParams(
            collective_id=0, has_side_effects=True, vmem_limit_bytes=61 * 2**20 + 768 * 2**10
        ),
    )(
        queries, keys, values, memory_init, norm_init, gate_logits.reshape(1, -1),
        dec_queries.transpose(1, 0, 2), cache_keys, cache_values,
        new_keys.transpose(1, 0, 2), new_values.transpose(1, 0, 2), cache_lengths,
    )
    return prefill, decoded.transpose(1, 0, 2)


def solution(mesh):
    rows = ("seq", "grp")
    every = ("seq", "head", "grp")
    in_specs = (
        P(rows, "head"),
        P(rows, "head"),
        P(rows, "head"),
        P("head", None, None),
        P("head", None),
        P(),
        P(every, None, None),
        P(every, None, None),
        P(every, None, None),
        P(every, None, None),
        P(every, None, None),
        P(every),
    )
    out_specs = (P(rows, "head"), P(every, None, None))
    return jax.shard_map(
        on_device, mesh=mesh, in_specs=in_specs, out_specs=out_specs, check_vma=False
    )
```

```python
import functools
import math

import jax
import jax.numpy as jnp
from jax import lax
from jax.experimental import pallas as pl
from jax.experimental.pallas import tpu as pltpu
from jax.sharding import PartitionSpec as P

MESH = pl.DeviceIdType.MESH
BF = jnp.bfloat16
F32 = jnp.float32

D = 128
ROWS = 512
G = 8
KH = 2
NK = 8
STEPS = 3
CACHE = 512
OWN = 8
YS = 4
HEADS = 4
SL = D // OWN
B2 = KH * SL + 8
B4 = KH * D + 16
CHUNKS = 2
CH = ROWS // CHUNKS
AHEAD = 2
UNROLL = 8
LOG2E = 1.4426950408889634
C = LOG2E / math.sqrt(D)
NEG = -1e30


def dot(a, b):
    return lax.dot_general(a, b, (((1,), (0,)), ((), ())), preferred_element_type=F32)


def dot_nt(a, b):
    return lax.dot_general(a, b, (((1,), (1,)), ((), ())), preferred_element_type=F32)


def dot_tn(a, b):
    return lax.dot_general(a, b, (((0,), (0,)), ((), ())), preferred_element_type=F32)


def lift(x):
    return jnp.where(x > 0, x + 1.0, jnp.exp(jnp.minimum(x, 0.0)))


def split(x):
    hi = x.astype(BF)
    return hi, (x - hi.astype(F32)).astype(BF)


def inverse(x):
    r = pl.reciprocal(x, approx=True)
    r = r * (2.0 - x * r)
    return r * (2.0 - x * r)


def lanes(s):
    return [s[:, i * D : (i + 1) * D] for i in range(s.shape[1] // D)]


def row_max(tiles):
    top = functools.reduce(jnp.maximum, tiles)
    return jnp.broadcast_to(jnp.max(top, axis=1, keepdims=True), top.shape)


def weights_of(tiles, top):
    shift = top * C
    return jnp.concatenate([jnp.exp2(t * C - shift).astype(BF) for t in tiles], axis=1)


def each(count, unroll, body):
    def some(i, carry):
        for u in range(unroll):
            body(i * unroll + u)
        return carry

    if count == unroll:
        some(0, 0)
    else:
        lax.fori_loop(0, count // unroll, some, 0)


def kernel(
    q_hbm, k_hbm, v_hbm, mem_init, norm_init, gates, dq, ck_hbm, cv_hbm, nk, nv, lengths,
    out, dec_out,
    q, kv, kve, ck, cv,
    acc, den, top, ret,
    gm, gd, qd, nf, fk, fv, dloc,
    pf, snd0, r0, snd1, r1, snd2, r2, snd3, r3, snd4, r4, r5, prior, pnorm,
    lsem, kvs, kvr, s0, rs0, s1, rs1, s2, rs2, s3, rs3, s4, rs4, s5, rs5,
):
    seq = lax.axis_index("seq")
    head = lax.axis_index("head")
    grp = lax.axis_index("grp")
    y = seq // OWN
    o = seq % OWN

    loads = []
    for j in range(KH):
        cols = pl.ds(j * D, D)
        loads.append(pltpu.make_async_copy(k_hbm.at[:, cols], kv.at[j, :, 0:D], lsem.at[j]))
        loads.append(
            pltpu.make_async_copy(v_hbm.at[:, cols], kv.at[j, :, D : 2 * D], lsem.at[KH + j])
        )
    load_q = pltpu.make_async_copy(q_hbm, q, lsem.at[4])
    load_ck = pltpu.make_async_copy(ck_hbm, ck, lsem.at[5])
    load_cv = pltpu.make_async_copy(cv_hbm, cv, lsem.at[6])
    for copy in loads:
        copy.start()
    load_q.start()
    load_ck.start()
    load_cv.start()

    def grp_peer():
        return {"grp": 1 - grp}

    def row_peer(n):
        return {"seq": y * OWN + (o + n) % OWN}

    def y_peer(n):
        return {"seq": ((y + n) % YS) * OWN + o}

    def head_peer(n):
        return {"head": (head + n) % HEADS}

    peers = [grp_peer()]
    peers += [row_peer(n) for n in range(1, OWN)]
    peers += [y_peer(n) for n in range(1, YS)]
    peers += [head_peer(n) for n in range(1, HEADS)]
    barrier = pltpu.get_barrier_semaphore()
    for peer in peers:
        pl.semaphore_signal(barrier, inc=1, device_id=peer, device_id_type=MESH)

    for j in range(KH):
        kv[j, :, 2 * D :] = jnp.ones((ROWS, D), BF)
        kve[j, :, 2 * D :] = jnp.ones((ROWS, D), BF)
    for copy in loads:
        copy.wait()

    row16 = lax.broadcasted_iota(jnp.int32, (16, D), 0)
    norm_rows = jnp.zeros((16, D), F32)
    for j in range(KH):
        lifted = lift(kv[j, :, 0:D].astype(F32)).astype(BF)
        pf[j * D : (j + 1) * D, :] = dot_tn(lifted, kv[j, :, D : 2 * D])
        norm_rows = norm_rows + jnp.where(
            row16 == j, dot(jnp.ones((16, ROWS), BF), lifted), 0.0
        )
    pf[KH * D :, :] = norm_rows
    snd0[...] = pf[...].astype(BF)

    pl.semaphore_wait(barrier, len(peers))

    def copy0():
        return pltpu.make_async_remote_copy(
            snd0, r0, s0.at[0], rs0.at[0], device_id=grp_peer(), device_id_type=MESH
        )

    copy0().start()

    def kv_copy(c):
        j = c // CHUNKS
        rows = pl.ds(c % CHUNKS * CH, CH)
        return pltpu.make_async_remote_copy(
            kv.at[j, rows, 0 : 2 * D], kve.at[j, rows, 0 : 2 * D], kvs.at[c], kvr.at[c],
            device_id=grp_peer(), device_id_type=MESH,
        )

    def pump(c):
        if c < KH * CHUNKS:

            @pl.when(grp == 0)
            def _():
                kv_copy(c - AHEAD).wait_send()
                kv_copy(c).start()

    def kv_arrived(j, first, last):
        for c in range(j * CHUNKS + first // CH, j * CHUNKS + last // CH):
            kv_copy(c).wait_recv()

    logits = gates[...]
    sig = 1.0 / (1.0 + jnp.exp(-logits))
    at = lax.broadcasted_iota(jnp.int32, (NK * G, NK * G), 0)
    col = lax.broadcasted_iota(jnp.int32, (NK * G, NK * G), 1)
    gm[...] = jnp.broadcast_to(
        jnp.sum(jnp.where(at == col, sig, 0.0), axis=1, keepdims=True), (NK * G, D)
    )
    at = lax.broadcasted_iota(jnp.int32, (NK * G * 4, NK * G), 0)
    col = lax.broadcasted_iota(jnp.int32, (NK * G * 4, NK * G), 1)
    own_row = (at >= col * 4) & (at < col * 4 + 4)
    gd[...] = jnp.broadcast_to(
        jnp.sum(jnp.where(own_row, sig, 0.0), axis=1, keepdims=True), (NK * G * 4, D)
    )

    load_q.wait()

    half = ROWS // 2
    halves = [pl.ds(b * half, half) for b in range(2)]
    r_at = lax.broadcasted_iota(jnp.int32, (half, D), 0)
    c_at = lax.broadcasted_iota(jnp.int32, (half, D), 1)

    def head_lane(h):
        return pl.ds(h * D if isinstance(h, int) else pl.multiple_of(h * D, D), D)

    def own_rows(j):
        def one(gi):
            h = j * G + gi
            queries = [q[rows, head_lane(h)] for rows in halves]
            results = []
            for b in range(2):
                seen = pl.ds(0, (b + 1) * half)
                tiles = lanes(dot_nt(queries[b], kv[j, seen, 0:D]))
                n = len(tiles)
                for i in range(2):
                    tiles[n - 2 + i] = jnp.where(c_at + i * D <= r_at, tiles[n - 2 + i], NEG)
                m = row_max(tiles)
                results.append((m, dot(weights_of(tiles, m), kv[j, seen, D:])))
            for rows, (m, res) in zip(halves, results):
                acc[h, rows, :] = res[:, :D]
                den[h, rows, :] = res[:, D:]
                top[h, rows, :] = m

        each(G, UNROLL, one)

    def square(j, first, last, store):
        seen = pl.ds(first, last - first)

        def one(gi):
            h = j * G + gi
            queries = [q[rows, head_lane(h)] for rows in halves]
            tops = [top[h, rows, :] for rows in halves]
            results = []
            for b in range(2):
                tiles = lanes(dot_nt(queries[b], kve[j, seen, 0:D]))
                m = jnp.maximum(row_max(tiles), tops[b])
                res = dot(weights_of(tiles, m), kve[j, seen, D:])
                fade = jnp.exp2((tops[b] - m) * C)
                results.append((m, fade, res))
            results = [
                (m, acc[h, rows, :] * fade + res[:, :D], den[h, rows, :] * fade + res[:, D:])
                for rows, (m, fade, res) in zip(halves, results)
            ]
            store(h, results)

        each(G, UNROLL, one)

    def keep(h, results):
        for rows, (m, numer, denom) in zip(halves, results):
            acc[h, rows, :] = numer
            den[h, rows, :] = denom
            top[h, rows, :] = m

    def gate_of(h):
        return gm[pl.ds(head * KH * G + h, 1), :]

    def finish(h, results):
        gate = gate_of(h)
        parts = [ret[h, rows, :] for rows in halves]
        for rows, part, (m, numer, denom) in zip(halves, parts, results):
            out[rows, head_lane(h)] = (part + (1.0 - gate) * numer * inverse(denom)).astype(BF)

    own_rows(0)

    copy0().wait_send()

    @pl.when(grp == 0)
    def _():
        for c in range(AHEAD):
            kv_copy(c).start()


    copy0().wait_recv()
    for t in range(OWN):
        for j in range(KH):
            rows = pl.ds(j * D + t * SL, SL)
            snd1[t, j * SL : (j + 1) * SL, :] = pf[rows, :] + r0[rows, :].astype(F32)
        snd1[t, KH * SL :, :] = (pf[KH * D :, :] + r0[KH * D :, :].astype(F32))[0:8]
    r1[o] = snd1[o]

    def send1(n):
        return pltpu.make_async_remote_copy(
            snd1.at[(o + n) % OWN], r1.at[o], s1.at[n], rs1.at[n], device_id=row_peer(n), device_id_type=MESH
        )

    def recv1(n):
        return pltpu.make_async_remote_copy(
            snd1.at[o], r1.at[(o + OWN - n) % OWN], s1.at[n], rs1.at[n],
            device_id=row_peer(n), device_id_type=MESH,
        )

    for n in range(1, OWN):
        send1(n).start()

    own_rows(1)

    for n in range(1, OWN):
        recv1(n).wait_recv()
    run = jnp.zeros((B2, D), F32)
    for t in range(OWN):
        snd3[t] = run[0 : KH * SL]
        run = run + r1[t]
    snd2[...] = run
    r2[y] = run

    def send2(n):
        return pltpu.make_async_remote_copy(
            snd2, r2.at[y], s2.at[n], rs2.at[n], device_id=y_peer(n), device_id_type=MESH
        )

    def recv2(n):
        return pltpu.make_async_remote_copy(
            snd2, r2.at[(y + YS - n) % YS], s2.at[n], rs2.at[n], device_id=y_peer(n), device_id_type=MESH
        )

    for n in range(1, YS):
        send2(n).start()

    qd[...] = jnp.zeros_like(qd)
    fk[...] = jnp.zeros_like(fk)
    fv[...] = jnp.zeros_like(fv)
    nf[...] = jnp.zeros_like(nf)
    for t in range(STEPS):
        for h in range(NK * G):
            j, gi = divmod(h, G)
            two = dq[t, :, h * D : (h + 1) * D].astype(F32)
            for r in range(2):
                qd[j, r * 32 + gi * 4 + t : r * 32 + gi * 4 + t + 1, :] = two[r : r + 1]
    for fresh, wide in ((nk, fk), (nv, fv)):
        for t in range(STEPS):
            two = fresh[t].astype(F32)
            for r in range(2):
                nf[r, t : t + 1, :] = two[r : r + 1]
        for r in range(2):
            wide[r, 0:16, :] = nf[r].astype(BF)
    load_ck.wait()
    load_cv.wait()

    c64 = lax.broadcasted_iota(jnp.int32, (64, D), 1)
    t64 = lax.broadcasted_iota(jnp.int32, (64, D), 0) % 4
    fresh_ok = (c64 <= t64) & (c64 < STEPS)

    def decode(r):
        length = lengths[r]

        def one(p):
            lane = pl.ds(p * 2 * D, 2 * D)
            none = jnp.zeros((32, D), BF)
            q0 = qd[2 * p, 32 * r : 32 * r + 32, :].astype(BF)
            q1 = qd[2 * p + 1, 32 * r : 32 * r + 32, :].astype(BF)
            both = jnp.concatenate(
                [jnp.concatenate([q0, none], axis=1), jnp.concatenate([none, q1], axis=1)], axis=0
            )
            tiles = lanes(dot_nt(both, ck[r, :, lane]))
            tiles = [jnp.where(c64 + i * D < length, s, NEG) for i, s in enumerate(tiles)]
            tiles.append(jnp.where(fresh_ok, dot_nt(both, fk[r, :, lane]), NEG))
            shift = row_max(tiles) * C
            ws = [jnp.exp2(s * C - shift) for s in tiles]
            tot = jnp.sum(functools.reduce(jnp.add, ws), axis=1, keepdims=True)
            ws = [w.astype(BF) for w in ws]
            res = dot(jnp.concatenate(ws[:-1], axis=1), cv[r, :, lane]) + dot(ws[-1], fv[r, :, lane])
            res = res / tot
            dloc[2 * p, 32 * r : 32 * r + 32, :] = res[0:32, 0:D]
            dloc[2 * p + 1, 32 * r : 32 * r + 32, :] = res[32:64, D:]

        each(NK // 2, NK // 2, one)

    decode(0)

    for n in range(1, YS):
        recv2(n).wait_recv()
    base = jnp.zeros((B2, D), F32)
    total = jnp.zeros((B2, D), F32)
    for t in range(YS):
        base = base + jnp.where(t < y, r2[t], 0.0)
        total = total + r2[t]
    for t in range(OWN):
        snd3[t] = snd3[t] + base[0 : KH * SL]
    r3[o] = snd3[o]

    def send3(n):
        return pltpu.make_async_remote_copy(
            snd3.at[(o + n) % OWN], r3.at[o], s3.at[n], rs3.at[n], device_id=row_peer(n), device_id_type=MESH
        )

    def recv3(n):
        return pltpu.make_async_remote_copy(
            snd3.at[o], r3.at[(o + OWN - n) % OWN], s3.at[n], rs3.at[n],
            device_id=row_peer(n), device_id_type=MESH,
        )

    for n in range(1, OWN):
        send3(n).start()

    row8 = lax.broadcasted_iota(jnp.int32, (8, D), 0)
    init8 = jnp.zeros((8, D), F32)
    for j in range(KH):
        init8 = init8 + jnp.where(row8 == j, norm_init[j : j + 1, :], 0.0)
    before = base[KH * SL :] + init8
    for t in range(OWN):
        before = before + jnp.where(t < o, r1[t, KH * SL :, :], 0.0)
    pnorm[...] = before
    for j in range(KH):
        init = mem_init[j, pl.ds(pl.multiple_of(o * SL, SL), SL), :]
        snd4[j * SL : (j + 1) * SL, :] = (total[j * SL : (j + 1) * SL] + init).astype(BF)
    snd4[KH * SL :, :] = jnp.concatenate(
        [total[KH * SL :] + init8, jnp.zeros((8, D), F32)], axis=0
    ).astype(BF)
    r4[head] = snd4[...]

    def send4(n):
        return pltpu.make_async_remote_copy(
            snd4, r4.at[head], s4.at[n], rs4.at[n], device_id=head_peer(n), device_id_type=MESH
        )

    def recv4(n):
        return pltpu.make_async_remote_copy(
            snd4, r4.at[(head + HEADS - n) % HEADS], s4.at[n], rs4.at[n],
            device_id=head_peer(n), device_id_type=MESH,
        )

    for n in range(1, HEADS):
        send4(n).start()
    pump(AHEAD)

    decode(1)
    pump(AHEAD + 1)

    for n in range(1, OWN):
        recv3(n).wait_recv()
    for j in range(KH):
        for t in range(OWN):
            at_d = pl.ds(t * SL, SL)
            prior[j, at_d, :] = r3[t, j * SL : (j + 1) * SL, :] + mem_init[j, at_d, :]

    def retrieve(j, last):
        m_hi, m_lo = split(prior[j])
        wide = jnp.concatenate([m_hi, m_lo], axis=1)
        numer_w = jnp.concatenate([wide, wide], axis=0)
        n_hi, n_lo = split(jnp.broadcast_to(pnorm[j : j + 1, :], (D, D)))
        tall = jnp.concatenate([n_hi, n_lo], axis=0)
        denom_w = jnp.concatenate([tall, tall], axis=1)

        def one(gi):
            h = j * G + gi
            gate = gate_of(h)
            queries = [q[rows, head_lane(h)] for rows in halves]
            if last:
                local = [(acc[h, rows, :], den[h, rows, :]) for rows in halves]
            results = []
            for b in range(2):
                hi, lo = split(lift(queries[b].astype(F32)))
                pair = jnp.concatenate([hi, lo], axis=1)
                numer = dot(pair, numer_w)
                denom = dot_nt(pair, denom_w)
                got = (numer[:, :D] + numer[:, D:]) * inverse(denom[:, :D] + denom[:, D:]) * gate
                if last:
                    got = got + (1.0 - gate) * local[b][0] * inverse(local[b][1])
                results.append(got)
            for rows, got in zip(halves, results):
                if last:
                    out[rows, head_lane(h)] = got.astype(BF)
                else:
                    ret[h, rows, :] = got

        each(G, UNROLL, one)

    def send5(n):
        return pltpu.make_async_remote_copy(
            r4.at[:, 0 : KH * SL, :], r5.at[o], s5.at[n], rs5.at[n],
            device_id=row_peer(n), device_id_type=MESH,
        )

    def recv5(n):
        return pltpu.make_async_remote_copy(
            r4.at[:, 0 : KH * SL, :], r5.at[(o + OWN - n) % OWN], s5.at[n], rs5.at[n],
            device_id=row_peer(n), device_id_type=MESH,
        )

    def pass_on():
        for n in range(1, HEADS):
            recv4(n).wait_recv()
        r5[o] = r4[:, 0 : KH * SL, :]
        for n in range(1, OWN):
            send5(n).start()


    @pl.when(grp == 0)
    def _():
        pass_on()
        for j in range(KH):
            retrieve(j, True)

    @pl.when(grp == 1)
    def _():
        for j in range(KH):
            retrieve(j, False)
        pass_on()

    @pl.when(grp == 1)
    def _():
        kv_arrived(0, 0, ROWS)
        square(0, 0, ROWS, finish)
        kv_arrived(1, 0, half)
        square(1, 0, half, keep)

    for n in range(1, OWN):
        recv5(n).wait_recv()
    for j in range(NK):
        at_s = (j % KH) * SL
        m_one = jnp.concatenate([r5[t, j // KH, at_s : at_s + SL, :] for t in range(OWN)], axis=0)
        numer_w = jnp.concatenate([m_one, m_one], axis=0)
        n_rows = r4[j // KH, KH * SL :, :].astype(F32)
        n_one = jnp.broadcast_to(n_rows[j % KH : j % KH + 1, :], (D, D)).astype(BF)
        denom_w = jnp.concatenate([n_one, n_one], axis=1)
        hi, lo = split(lift(qd[j]))
        pair = jnp.concatenate([hi, lo], axis=1)
        got = dot(pair, numer_w) * inverse(dot_nt(pair, denom_w))
        gate = gd[j * G * 4 : (j + 1) * G * 4, :]
        gate = jnp.concatenate([gate, gate], axis=0)
        mixed = gate * got + (1.0 - gate) * dloc[j]
        for gi in range(G):
            at_h = (j * G + gi) * D
            for t in range(STEPS):
                row = gi * 4 + t
                dec_out[t, :, at_h : at_h + D] = jnp.concatenate(
                    [mixed[row : row + 1], mixed[32 + row : 33 + row]], axis=0
                ).astype(BF)

    @pl.when(grp == 1)
    def _():
        kv_arrived(1, half, ROWS)
        square(1, half, ROWS, finish)

    @pl.when(grp == 0)
    def _():
        for c in range(KH * CHUNKS - AHEAD, KH * CHUNKS):
            kv_copy(c).wait_send()

    for n in range(1, OWN):
        send1(n).wait_send()
    for n in range(1, YS):
        send2(n).wait_send()
    for n in range(1, OWN):
        send3(n).wait_send()
    for n in range(1, HEADS):
        send4(n).wait_send()
    for n in range(1, OWN):
        send5(n).wait_send()


def on_device(
    queries, keys, values, memory_init, norm_init, gate_logits,
    dec_queries, cache_keys, cache_values, new_keys, new_values, cache_lengths,
):
    hbm = pl.BlockSpec(memory_space=pltpu.HBM)
    vmem = pl.BlockSpec(memory_space=pltpu.VMEM)
    smem = pl.BlockSpec(memory_space=pltpu.SMEM)
    V = pltpu.VMEM
    DMA = pltpu.SemaphoreType.DMA
    prefill, decoded = pl.pallas_call(
        kernel,
        out_shape=(
            V((ROWS, KH * G * D), BF),
            V((STEPS, 2, NK * G * D), BF),
        ),
        in_specs=[hbm, hbm, hbm, vmem, vmem, vmem, vmem, hbm, hbm, vmem, vmem, smem],
        out_specs=(vmem, vmem),
        scratch_shapes=[
            V((ROWS, KH * G * D), BF),
            V((KH, ROWS, 3 * D), BF),
            V((KH, ROWS, 3 * D), BF),
            V((2, CACHE, NK * D), BF),
            V((2, CACHE, NK * D), BF),
            V((KH * G, ROWS, D), F32),
            V((KH * G, ROWS, D), F32),
            V((KH * G, ROWS, D), F32),
            V((KH * G, ROWS, D), F32),
            V((NK * G, D), F32),
            V((NK * G * 4, D), F32),
            V((NK, 64, D), F32),
            V((2, 16, NK * D), F32),
            V((2, D, NK * D), BF),
            V((2, D, NK * D), BF),
            V((NK, 64, D), F32),
            V((B4, D), F32),
            V((B4, D), BF),
            V((B4, D), BF),
            V((OWN, B2, D), F32),
            V((OWN, B2, D), F32),
            V((B2, D), F32),
            V((YS, B2, D), F32),
            V((OWN, KH * SL, D), F32),
            V((OWN, KH * SL, D), F32),
            V((KH * SL + 16, D), BF),
            V((HEADS, KH * SL + 16, D), BF),
            V((OWN, HEADS, KH * SL, D), BF),
            V((KH, D, D), F32),
            V((8, D), F32),
            DMA((7,)), DMA((KH * CHUNKS,)), DMA((KH * CHUNKS,)), DMA((1,)), DMA((1,)),
            DMA((OWN,)), DMA((OWN,)), DMA((YS,)), DMA((YS,)),
            DMA((OWN,)), DMA((OWN,)), DMA((HEADS,)), DMA((HEADS,)),
            DMA((OWN,)), DMA((OWN,)),
        ],
        compiler_params=pltpu.CompilerParams(
            collective_id=0, has_side_effects=True, vmem_limit_bytes=61 * 2**20 + 768 * 2**10
        ),
    )(
        queries, keys, values, memory_init, norm_init, gate_logits.reshape(1, -1),
        dec_queries.transpose(1, 0, 2), cache_keys, cache_values,
        new_keys.transpose(1, 0, 2), new_values.transpose(1, 0, 2), cache_lengths,
    )
    return prefill, decoded.transpose(1, 0, 2)


def solution(mesh):
    rows = ("seq", "grp")
    every = ("seq", "head", "grp")
    in_specs = (
        P(rows, "head"),
        P(rows, "head"),
        P(rows, "head"),
        P("head", None, None),
        P("head", None),
        P(),
        P(every, None, None),
        P(every, None, None),
        P(every, None, None),
        P(every, None, None),
        P(every, None, None),
        P(every),
    )
    out_specs = (P(rows, "head"), P(every, None, None))
    return jax.shard_map(
        on_device, mesh=mesh, in_specs=in_specs, out_specs=out_specs, check_vma=False
    )
```
